32 devices in a mesh: parts: 2 (over y), lat: 8 (over z, x), sub: 2 (over core).
Axes of the slice: x: 2, y: 2, z: 4, core: 2. Of those that a mesh axis runs over, the one named last changes fastest.
Arguments:
- residuals: bfloat16 [64, 5120], P(('parts', 'lat', 'sub')), parts along dimension 0, may hold values from -6 to 6
- enc_weight: bfloat16 [5120, 8192], P(None, ('parts', 'lat', 'sub')), parts along dimension 1, may hold values from -0.078125 to 0.078125
- enc_bias: float32 [8192], P(('parts', 'lat', 'sub')), parts along dimension 0, may hold values from -0.5 to 0.5
- dec_weight: bfloat16 [8192, 5120], P(('parts', 'lat', 'sub')), parts along dimension 0, may hold values from -0.1875 to 0.1875
- dec_bias: float32 [10240], P('parts'), parts along dimension 0, may hold values from -3 to 3
Outputs:
- reconstruction: bfloat16 [64, 5120], P(('parts', 'lat', 'sub')), parts along dimension 0
- loss_value: float32 [2], P('parts'), parts along dimension 0
- grad_enc: bfloat16 [5120, 8192], P(None, ('parts', 'lat', 'sub')), parts along dimension 1
- grad_enc_bias: float32 [8192], P(('parts', 'lat', 'sub')), parts along dimension 0
- grad_dec: bfloat16 [8192, 5120], P(('parts', 'lat', 'sub')), parts along dimension 0
- grad_dec_bias: float32 [10240], P('parts'), parts along dimension 0
The draws below stay inside these ranges and needn't reach their ends.
There are 2 independent parts, one for each index of `parts`. The reference program is written for one: setup_inputs(seed, part) draws one part's arguments, and reference() takes and returns one part's arrays. A program takes and returns all parts, laid end to end along the dimension named above; each array names one. Nothing has to cross between parts.
All inputs are finite; a program needn't handle non-finite values.
Results may differ from the reference program's by a relative error of at most 0.00155.
The reference program's roundings to bfloat16 on the way (of `centered`, `codes_bf` and `resid_bf`) count: a program that leaves them out, or rounds other values in their place, can miss the bound.
Values may be sent and summed in bfloat16 or wider, within the bound.
No kernel may reach another device: no remote copies, remote signals or barrier semaphores. Data moves between devices by JAX's collectives and lax.ppermute only.
A program may use at most 128 MiB of HBM per device.

```python
import jax
import jax.numpy as jnp
from jax import lax

D = 5120
LATENTS = 4096
ROWS = 32


def block_levels(own_key, dims, cuts, smallest, top_value):
    factor_of = 1.0
    for position, shards_of in cuts:
        heights = jax.random.uniform(jax.random.fold_in(jax.random.fold_in(own_key, 6), position), (shards_of,), jnp.float32, smallest / len(cuts), top_value / len(cuts))
        factor_of = factor_of * jnp.repeat(jnp.exp(heights), dims[position] // shards_of).reshape((-1,) + (1,) * (len(dims) - 1 - position))
    return factor_of


def noise(stream_key, shape, deviation, limit, pieces=(), kind=jnp.bfloat16):
    loudness = block_levels(stream_key, shape, pieces, -0.22, 0.18) if pieces else 1.0
    drawn = jax.random.normal(stream_key, shape, jnp.float32) * deviation * loudness
    return jnp.minimum(jnp.maximum(drawn, -limit), limit).astype(kind)


def setup_inputs(seed: int = 0, part: int = 0) -> dict:
    keys = jax.random.split(jax.random.key(seed), 6)
    part_splits = jax.random.split(jax.random.fold_in(keys[5], part), 6)
    residuals = noise(part_splits[0], (ROWS, D), 1.0, 6.0, ((0, 16),))
    enc_weight = noise(part_splits[1], (D, LATENTS), D ** -0.5, 0.078125, ((1, 16),))
    enc_bias = jnp.clip(jax.random.uniform(part_splits[2], (LATENTS,), jnp.float32, -0.5, 0.5) * block_levels(part_splits[2], (LATENTS,), ((0, 16),), -0.4, 0.0), -0.5, 0.5)
    dec_weight = noise(part_splits[3], (LATENTS, D), (LATENTS // 4) ** -0.5, 0.1875, ((0, 16),))
    dec_bias = noise(part_splits[4], (D,), 0.5, 3.0, (), jnp.float32)
    return {"residuals": residuals, "enc_weight": enc_weight, "enc_bias": enc_bias, "dec_weight": dec_weight, "dec_bias": dec_bias}


PENALTY = 0.2


def reference(residuals, enc_weight, enc_bias, dec_weight, dec_bias):
    row_count = residuals.shape[0]
    width = residuals.shape[1]
    inputs_f = residuals.astype(jnp.float32)
    centered = (inputs_f - dec_bias).astype(jnp.bfloat16)
    preact = jnp.dot(centered, enc_weight, preferred_element_type=jnp.float32) + enc_bias
    active = jnp.maximum(preact, 0.0)
    codes = active * active
    codes_bf = codes.astype(jnp.bfloat16)
    recon_f = jnp.dot(codes_bf, dec_weight, preferred_element_type=jnp.float32) + dec_bias
    error_rows = recon_f - inputs_f
    total = (jnp.sum(error_rows * error_rows) + PENALTY * jnp.sum(codes)) / row_count
    loss_value = jnp.reshape(total / width, (1,))
    resid_grad = (2.0 / row_count) * error_rows
    resid_bf = resid_grad.astype(jnp.bfloat16)
    grad_dec = lax.dot_general(codes_bf, resid_bf, (((0,), (0,)), ((), ())), preferred_element_type=jnp.float32).astype(jnp.bfloat16)
    back_codes = lax.dot_general(resid_bf, dec_weight, (((1,), (1,)), ((), ())), preferred_element_type=jnp.float32)
    code_grad = 2.0 * active * (back_codes + PENALTY / row_count)
    grad_enc = lax.dot_general(centered, code_grad.astype(jnp.bfloat16), (((0,), (0,)), ((), ())), preferred_element_type=jnp.float32).astype(jnp.bfloat16)
    grad_enc_bias = jnp.sum(code_grad, axis=0)
    grad_dec_bias = jnp.sum(resid_grad, axis=0) - jnp.dot(enc_weight.astype(jnp.float32), grad_enc_bias, precision=lax.Precision.HIGHEST)
    return recon_f.astype(jnp.bfloat16), loss_value, grad_enc, grad_enc_bias, grad_dec, grad_dec_bias
```

```python
import jax
import jax.numpy as jnp
from jax import lax
from jax.sharding import PartitionSpec as P

PENALTY = 0.2
CORES = 0


def swap(values, mask):
    if mask == CORES:
        return lax.ppermute(values, "sub", [(i, i ^ 1) for i in range(2)])
    return lax.ppermute(values, "lat", [(i, i ^ mask) for i in range(lax.axis_size("lat"))])


def gather(rows, masks):
    for mask in masks:
        rows = jnp.concatenate([rows, swap(rows, mask)], axis=0)
    return rows


def halve(rows, masks):
    for mask in masks:
        half = rows.shape[0] // 2
        rows = rows[:half] + swap(rows[half:], mask)
    return rows


def local(residuals, enc_weight, enc_bias, dec_weight, dec_bias):
    own_rows, width = residuals.shape
    lat = lax.axis_size("lat")
    row_count = own_rows * lat * lax.axis_size("sub")
    bits = [1 << b for b in range(lat.bit_length() - 1)]
    far, near = bits[-1], bits[:-1]

    paired = gather(residuals, [far])
    gathered = gather(paired, near[::-1] + [CORES])
    centered = (gathered.astype(jnp.float32) - dec_bias).astype(jnp.bfloat16)
    preact = jnp.dot(centered, enc_weight, preferred_element_type=jnp.float32) + enc_bias
    active = jnp.maximum(preact, 0.0)
    codes = active * active
    codes_bf = codes.astype(jnp.bfloat16)
    code_total = jnp.sum(codes)

    partial = jnp.dot(codes_bf, dec_weight, preferred_element_type=jnp.float32)
    summed = halve(partial, [CORES] + near)
    other = swap(summed, far)
    summed = summed + jnp.concatenate([other[own_rows:], other[:own_rows]], axis=0)
    recon_f = summed + dec_bias
    error_rows = recon_f - paired.astype(jnp.float32)
    resid_grad = 2.0 / row_count * error_rows
    resid_bf = resid_grad.astype(jnp.bfloat16)
    own_error = error_rows[:own_rows]
    sq_total = jnp.sum(own_error * own_error)
    own_bias = jnp.sum(resid_grad[:own_rows], axis=0)

    resid_all = gather(resid_bf, near[::-1] + [CORES])
    back_codes = lax.dot_general(
        resid_all, dec_weight, (((1,), (1,)), ((), ())), preferred_element_type=jnp.float32
    )
    code_grad = 2.0 * active * (back_codes + PENALTY / row_count)
    grad_enc_bias = jnp.sum(code_grad, axis=0)
    bias_terms = own_bias - jnp.dot(
        enc_weight.astype(jnp.float32), grad_enc_bias, precision=lax.Precision.HIGHEST
    )
    scalars = (sq_total + PENALTY * code_total) / row_count
    terms = jnp.concatenate([bias_terms, jnp.broadcast_to(scalars, (128,))])
    for mask in [CORES] + bits:
        terms = terms + swap(terms, mask)
    grad_dec = lax.dot_general(
        codes_bf, resid_all, (((0,), (0,)), ((), ())), preferred_element_type=jnp.float32
    ).astype(jnp.bfloat16)
    grad_enc = lax.dot_general(
        centered,
        code_grad.astype(jnp.bfloat16),
        (((0,), (0,)), ((), ())),
        preferred_element_type=jnp.float32,
    ).astype(jnp.bfloat16)
    return (
        recon_f[:own_rows].astype(jnp.bfloat16),
        terms[width : width + 1] / width,
        grad_enc,
        grad_enc_bias,
        grad_dec,
        terms[:width],
    )


def solution(mesh):
    placed = (
        P(("parts", "lat", "sub"), None),
        P(None, ("parts", "lat", "sub")),
        P(("parts", "lat", "sub")),
        P(("parts", "lat", "sub"), None),
        P("parts"),
    )
    return jax.shard_map(
        local,
        mesh=mesh,
        in_specs=placed,
        out_specs=(
            P(("parts", "lat", "sub"), None),
            P("parts"),
            P(None, ("parts", "lat", "sub")),
            P(("parts", "lat", "sub")),
            P(("parts", "lat", "sub"), None),
            P("parts"),
        ),
        check_vma=False,
    )
```

```python
import jax
import jax.numpy as jnp
from jax import lax
from jax.experimental import pallas as pl
from jax.experimental.pallas import tpu as pltpu
from jax.sharding import PartitionSpec as P

PENALTY = 0.2
CORES = 0
LANES = 128
VMEM = pl.BlockSpec(memory_space=pltpu.VMEM)


def swap(values, mask):
    if mask == CORES:
        return lax.ppermute(values, "sub", [(i, i ^ 1) for i in range(2)])
    return lax.ppermute(values, "lat", [(i, i ^ mask) for i in range(lax.axis_size("lat"))])


def plan(lat):
    bits = [1 << b for b in range(lat.bit_length() - 1)]
    near = bits[:-1]
    steps = [[1, 2, 3]] + [[b] for b in near[2:]] if len(near) > 1 else [[b] for b in near]
    return bits[-1], steps


def gather(rows, steps):
    for masks in steps:
        rows = jnp.concatenate([rows] + [swap(rows, mask) for mask in masks], axis=0)
        rows = lax.optimization_barrier(rows)
    return rows


def halve(rows, steps):
    for masks in steps:
        size = rows.shape[0] // (len(masks) + 1)
        parts = [rows[j * size : (j + 1) * size] for j in range(len(masks) + 1)]
        rows = parts[0] + sum(swap(part, mask) for part, mask in zip(parts[1:], masks))
    return rows


def encode_decode(half_a, half_b, enc_weight, enc_bias, dec_weight, dec_bias):
    half, width = half_a.shape
    latents = enc_weight.shape[1]

    def kernel(a_ref, b_ref, enc_ref, enc_bias_ref, dec_ref, dec_bias_ref, centered_ref, active_ref, codes_ref, keep_ref, send_ref):
        bias = dec_bias_ref[...]
        centered_ref[:half] = (a_ref[...].astype(jnp.float32) - bias).astype(jnp.bfloat16)
        centered_ref[half:] = (b_ref[...].astype(jnp.float32) - bias).astype(jnp.bfloat16)
        preact = jnp.dot(centered_ref[...], enc_ref[...], preferred_element_type=jnp.float32) + enc_bias_ref[...]
        active = jnp.maximum(preact, 0.0)
        active_ref[...] = active
        codes = (active * active).astype(jnp.bfloat16)
        codes_ref[...] = codes
        partial = jnp.dot(codes, dec_ref[...], preferred_element_type=jnp.float32)
        keep_ref[...] = partial[:half]
        send_ref[...] = partial[half:]

    return pl.pallas_call(
        kernel,
        out_shape=[
            jax.ShapeDtypeStruct((2 * half, width), jnp.bfloat16),
            jax.ShapeDtypeStruct((2 * half, latents), jnp.float32),
            jax.ShapeDtypeStruct((2 * half, latents), jnp.bfloat16),
            jax.ShapeDtypeStruct((half, width), jnp.float32),
            jax.ShapeDtypeStruct((half, width), jnp.float32),
        ],
        in_specs=[VMEM] * 6,
        out_specs=[VMEM] * 5,
        compiler_params=pltpu.CompilerParams(vmem_limit_bytes=40 << 20),
        name="encode_decode",
    )(half_a, half_b, enc_weight, enc_bias, dec_weight, dec_bias)


def backward(half_a, half_b, dec_weight, enc_weight, active, own_bias, row_count):
    half, width = half_a.shape
    latents = dec_weight.shape[0]
    contract_last = (((1,), (1,)), ((), ()))

    def kernel(a_ref, b_ref, dec_ref, enc_ref, active_ref, own_ref, code_grad_ref, enc_bias_ref, terms_ref):
        resid = jnp.concatenate([a_ref[...], b_ref[...]], axis=0)
        back = lax.dot_general(resid, dec_ref[...], contract_last, preferred_element_type=jnp.float32)
        code_grad = 2.0 * active_ref[...] * (back + PENALTY / row_count)
        code_grad_ref[...] = code_grad.astype(jnp.bfloat16)
        total = jnp.sum(code_grad, axis=0, keepdims=True)
        enc_bias_ref[...] = total
        high = total.astype(jnp.bfloat16)
        rest = total - high.astype(jnp.float32)
        middle = rest.astype(jnp.bfloat16)
        low = (rest - middle.astype(jnp.float32)).astype(jnp.bfloat16)
        pieces = jnp.concatenate([high, middle, low], axis=0)
        product = lax.dot_general(pieces, enc_ref[...], contract_last, preferred_element_type=jnp.float32)
        terms_ref[...] = own_ref[...] - (product[0:1] + (product[1:2] + product[2:3]))

    return pl.pallas_call(
        kernel,
        out_shape=[
            jax.ShapeDtypeStruct((2 * half, latents), jnp.bfloat16),
            jax.ShapeDtypeStruct((1, latents), jnp.float32),
            jax.ShapeDtypeStruct((1, width), jnp.float32),
        ],
        in_specs=[VMEM] * 6,
        out_specs=[VMEM] * 3,
        compiler_params=pltpu.CompilerParams(vmem_limit_bytes=40 << 20),
        name="backward",
    )(half_a, half_b, dec_weight, enc_weight, active, own_bias)


def local(residuals, enc_weight, enc_bias, dec_weight, dec_bias):
    own_rows, width = residuals.shape
    lat = lax.axis_size("lat")
    row_count = own_rows * lat * lax.axis_size("sub")
    far, steps = plan(lat)
    bias_row = dec_bias.reshape(1, width)

    paired = gather(residuals, [[far]])
    rows_a = gather(paired, steps)
    rows_b = swap(rows_a, CORES)
    centered, active, codes_bf, keep, send = encode_decode(
        rows_a, rows_b, enc_weight, enc_bias.reshape(1, -1), dec_weight, bias_row
    )

    summed = halve(keep + swap(send, CORES), steps[::-1])
    other = swap(summed, far)
    summed = summed + jnp.concatenate([other[own_rows:], other[:own_rows]], axis=0)
    recon_f = summed + dec_bias
    error_rows = recon_f - paired.astype(jnp.float32)
    resid_grad = 2.0 / row_count * error_rows
    resid_bf = resid_grad.astype(jnp.bfloat16)
    own_error = error_rows[:own_rows]
    sq_total = jnp.sum(own_error * own_error)
    own_bias = jnp.sum(resid_grad[:own_rows], axis=0, keepdims=True)
    code_total = jnp.sum(active * active)

    resid_a = gather(resid_bf, steps)
    resid_b = swap(resid_a, CORES)
    code_grad_bf, grad_enc_bias, bias_terms = backward(
        resid_a, resid_b, dec_weight, enc_weight, active, own_bias, row_count
    )
    scalars = (sq_total + PENALTY * code_total) / row_count
    terms = jnp.concatenate([bias_terms[0], jnp.broadcast_to(scalars, (LANES,))])
    for mask in [CORES] + [1 << b for b in range(lat.bit_length() - 1)]:
        terms = terms + swap(terms, mask)
    resid_all = jnp.concatenate([resid_a, resid_b], axis=0)
    grad_dec = lax.dot_general(
        codes_bf, resid_all, (((0,), (0,)), ((), ())), preferred_element_type=jnp.float32
    ).astype(jnp.bfloat16)
    grad_enc = lax.dot_general(
        centered, code_grad_bf, (((0,), (0,)), ((), ())), preferred_element_type=jnp.float32
    ).astype(jnp.bfloat16)
    return (
        recon_f[:own_rows].astype(jnp.bfloat16),
        terms[width : width + 1] / width,
        grad_enc,
        grad_enc_bias[0],
        grad_dec,
        terms[:width],
    )


def solution(mesh):
    placed = (
        P(("parts", "lat", "sub"), None),
        P(None, ("parts", "lat", "sub")),
        P(("parts", "lat", "sub")),
        P(("parts", "lat", "sub"), None),
        P("parts"),
    )
    return jax.shard_map(
        local,
        mesh=mesh,
        in_specs=placed,
        out_specs=(
            P(("parts", "lat", "sub"), None),
            P("parts"),
            P(None, ("parts", "lat", "sub")),
            P(("parts", "lat", "sub")),
            P(("parts", "lat", "sub"), None),
            P("parts"),
        ),
        check_vma=False,
    )
```

```python
import jax
import jax.numpy as jnp
from jax import lax
from jax.experimental import pallas as pl
from jax.experimental.pallas import tpu as pltpu
from jax.sharding import PartitionSpec as P

PENALTY = 0.2
CORES = 0
LANES = 128
LIMIT = 12 << 20
VMEM = pl.BlockSpec(memory_space=pltpu.VMEM)
HBM = pl.BlockSpec(memory_space=pltpu.HBM)
CONTRACT_FIRST = (((0,), (0,)), ((), ()))
CONTRACT_LAST = (((1,), (1,)), ((), ()))


def vmem(shape, dtype):
    return pltpu.VMEM(shape, dtype)


def in_vmem(array):
    return pltpu.with_memory_space_constraint(array, pltpu.VMEM)


def in_hbm(array):
    return pltpu.with_memory_space_constraint(array, pltpu.HBM)


TOKEN = ((8, LANES), jnp.float32)


def run(kernel, name, outs, args, after=(), flops=0, moved=0, limit=LIMIT):
    count = len(args)

    def body(*refs):
        kernel(*refs[:count], *refs[count + len(after) :])

    return pl.pallas_call(
        body,
        out_shape=[vmem(*out) for out in outs],
        in_specs=[VMEM] * (count + len(after)),
        out_specs=[VMEM] * len(outs),
        compiler_params=pltpu.CompilerParams(vmem_limit_bytes=limit),
        cost_estimate=pl.CostEstimate(flops=flops, bytes_accessed=moved, transcendentals=0),
        name=name,
    )(*[in_vmem(a) for a in args], *[in_vmem(a) for a in after])


def swap(values, mask):
    if mask == CORES:
        return lax.ppermute(values, "sub", [(i, i ^ 1) for i in range(2)])
    return lax.ppermute(values, "lat", [(i, i ^ mask) for i in range(lax.axis_size("lat"))])


def plan(lat):
    bits = [1 << b for b in range(lat.bit_length() - 1)]
    near = bits[:-1]
    steps = [[1, 2, 3]] + [[b] for b in near[2:]] if len(near) > 1 else [[b] for b in near]
    return bits[-1], steps


def load(arrays, after=()):
    count = len(arrays)

    def kernel(*refs):
        copies = [
            pltpu.make_async_copy(refs[i], refs[count + len(after) + i], refs[-1].at[i]) for i in range(count)
        ]
        for copy in copies:
            copy.start()
        for copy in copies:
            copy.wait()

    return pl.pallas_call(
        kernel,
        out_shape=[vmem(array.shape, array.dtype) for array in arrays],
        in_specs=[HBM] * count + [VMEM] * len(after),
        out_specs=[VMEM] * count,
        scratch_shapes=[pltpu.SemaphoreType.DMA((count,))],
        compiler_params=pltpu.CompilerParams(vmem_limit_bytes=LIMIT),
        cost_estimate=pl.CostEstimate(
            flops=0, bytes_accessed=2 * sum(a.size * a.dtype.itemsize for a in arrays), transcendentals=0
        ),
        name="load",
    )(*[in_hbm(a) for a in arrays], *[in_vmem(a) for a in after])


def stack(blocks, after=()):
    rows, width = blocks[0].shape

    def kernel(*refs):
        refs[-1][...] = jnp.concatenate([ref[...] for ref in refs[:-1]], axis=0)

    shape = (sum(block.shape[0] for block in blocks), width)
    return run(kernel, "stack", [(shape, blocks[0].dtype)], blocks, after)[0]


def gather(rows, steps, after=()):
    for masks in steps:
        rows = stack([rows] + [swap(rows, mask) for mask in masks], after)
    return rows


def add_parts(first, others, count):
    rows, width = first.shape
    size = rows // count

    def kernel(*refs):
        total = refs[0][...]
        for ref in refs[1 : 1 + len(others)]:
            total = total + ref[...]
        for part, ref in enumerate(refs[1 + len(others) :]):
            ref[...] = total[part * size : (part + 1) * size]

    return run(kernel, "add_parts", [((size, width), jnp.float32)] * count, [first, *others])


def halve(first, others, steps):
    for masks in steps:
        parts = add_parts(first, others, len(masks) + 1)
        first, others = parts[0], [swap(part, mask) for part, mask in zip(parts[1:], masks)]
    return add_parts(first, others, 1)[0]


def encode_decode(half_a, half_b, enc_weight, enc_bias, dec_weight, dec_bias):
    half, width = half_a.shape
    latents = enc_weight.shape[1]

    def kernel(a_ref, b_ref, enc_ref, enc_bias_ref, dec_ref, dec_bias_ref, centered_ref, active_ref, codes_ref, keep_ref, send_ref, sum_ref):
        bias = dec_bias_ref[...]
        centered_ref[:half] = (a_ref[...].astype(jnp.float32) - bias).astype(jnp.bfloat16)
        centered_ref[half:] = (b_ref[...].astype(jnp.float32) - bias).astype(jnp.bfloat16)
        preact = jnp.dot(centered_ref[...], enc_ref[...], preferred_element_type=jnp.float32) + enc_bias_ref[...]
        active = jnp.maximum(preact, 0.0)
        active_ref[...] = active
        codes = active * active
        codes_bf = codes.astype(jnp.bfloat16)
        codes_ref[...] = codes_bf
        partial = jnp.dot(codes_bf, dec_ref[...], preferred_element_type=jnp.float32)
        keep_ref[...] = partial[:half]
        send_ref[...] = partial[half:]
        sum_ref[...] = jnp.broadcast_to(jnp.sum(codes, keepdims=True), (1, LANES))

    return run(
        kernel,
        "encode_decode",
        [
            ((2 * half, width), jnp.bfloat16),
            ((2 * half, latents), jnp.float32),
            ((2 * half, latents), jnp.bfloat16),
            ((half, width), jnp.float32),
            ((half, width), jnp.float32),
            ((1, LANES), jnp.float32),
        ],
        [half_a, half_b, enc_weight, enc_bias, dec_weight, dec_bias],
    )


def residual_gradient(summed, other, paired, dec_bias, row_count):
    rows, width = summed.shape
    own = rows // 2

    def kernel(summed_ref, other_ref, paired_ref, bias_ref, recon_ref, resid_ref, own_ref, square_ref):
        total = summed_ref[...] + jnp.concatenate([other_ref[own:], other_ref[:own]], axis=0)
        recon = total + bias_ref[...]
        error = recon - paired_ref[...].astype(jnp.float32)
        grad = 2.0 / row_count * error
        recon_ref[...] = recon[:own].astype(jnp.bfloat16)
        resid_ref[...] = grad.astype(jnp.bfloat16)
        own_ref[...] = jnp.sum(grad[:own], axis=0, keepdims=True)
        square_ref[...] = jnp.broadcast_to(jnp.sum(error[:own] * error[:own], keepdims=True), (1, LANES))

    return run(
        kernel,
        "residual_gradient",
        [
            ((own, width), jnp.bfloat16),
            ((rows, width), jnp.bfloat16),
            ((1, width), jnp.float32),
            ((1, LANES), jnp.float32),
        ],
        [summed, other, paired, dec_bias],
    )


def backward(half_a, half_b, dec_weight, active, row_count):
    half, width = half_a.shape
    latents = dec_weight.shape[0]

    def kernel(a_ref, b_ref, dec_ref, active_ref, code_grad_ref, total_ref):
        resid = jnp.concatenate([a_ref[...], b_ref[...]], axis=0)
        back = lax.dot_general(resid, dec_ref[...], CONTRACT_LAST, preferred_element_type=jnp.float32)
        code_grad = 2.0 * active_ref[...] * (back + PENALTY / row_count)
        code_grad_ref[...] = code_grad.astype(jnp.bfloat16)
        total_ref[...] = jnp.sum(code_grad, axis=0, keepdims=True)

    return run(
        kernel,
        "backward",
        [((2 * half, latents), jnp.bfloat16), ((1, latents), jnp.float32)],
        [half_a, half_b, dec_weight, active],
    )


def bias_product(total, enc_weight, own_bias, square, code_sum, row_count):
    width, latents = enc_weight.shape

    def kernel(total_ref, enc_ref, own_ref, square_ref, sum_ref, terms_ref):
        values = total_ref[...]
        high = values.astype(jnp.bfloat16).astype(jnp.float32)
        rest = values - high
        middle = rest.astype(jnp.bfloat16).astype(jnp.float32)
        pieces = [high, middle, rest - middle, jnp.zeros((5, latents), jnp.float32)]
        pieces = jnp.concatenate(pieces, axis=0).astype(jnp.bfloat16)
        product = lax.dot_general(pieces, enc_ref[...], CONTRACT_LAST, preferred_element_type=jnp.float32)
        terms_ref[:, :width] = own_ref[...] - (product[0:1] + (product[1:2] + product[2:3]))
        terms_ref[:, width:] = (square_ref[...] + PENALTY * sum_ref[...]) / row_count

    return run(
        kernel,
        "bias_product",
        [((1, width + LANES), jnp.float32)],
        [total, enc_weight, own_bias, square, code_sum],
    )[0]


def dec_gradient(codes, resid_a, resid_b, recon, after, pieces=4):
    rows, latents = codes.shape
    half, width = resid_a.shape
    size = width // pieces

    def kernel(codes_ref, a_ref, b_ref, recon_ref, after_ref, grad_ref, recon_out_ref, token_ref, buffer, sems):
        recon_copy = pltpu.make_async_copy(recon_ref, recon_out_ref, sems.at[pieces])
        recon_copy.start()
        token_ref[...] = jnp.zeros_like(token_ref)
        turned = codes_ref[...].T
        copies = []
        for piece in range(pieces):
            columns = pl.ds(piece * size, size)
            resid = jnp.concatenate([a_ref[:, columns], b_ref[:, columns]], axis=0)
            buffer[:, columns] = jnp.dot(turned, resid, preferred_element_type=jnp.float32).astype(jnp.bfloat16)
            copies.append(pltpu.make_async_copy(buffer.at[:, columns], grad_ref.at[:, columns], sems.at[piece]))
            copies[-1].start()
        for copy in copies:
            copy.wait()
        recon_copy.wait()

    return pl.pallas_call(
        kernel,
        out_shape=[
            jax.ShapeDtypeStruct((latents, width), jnp.bfloat16),
            jax.ShapeDtypeStruct(recon.shape, jnp.bfloat16),
            vmem(*TOKEN),
        ],
        in_specs=[VMEM] * 5,
        out_specs=[HBM, HBM, VMEM],
        scratch_shapes=[pltpu.VMEM((latents, width), jnp.bfloat16), pltpu.SemaphoreType.DMA((pieces + 1,))],
        compiler_params=pltpu.CompilerParams(vmem_limit_bytes=LIMIT),
        cost_estimate=pl.CostEstimate(flops=2 * rows * latents * width, bytes_accessed=4 * latents * width, transcendentals=0),
        name="dec_gradient",
    )(*[in_vmem(a) for a in (codes, resid_a, resid_b, recon, after)])


def enc_gradient(centered, code_grad, total, after, pieces=4):
    rows, width = centered.shape
    latents = code_grad.shape[1]
    size = width // pieces

    def kernel(centered_ref, code_grad_ref, total_ref, after_ref, grad_ref, total_out_ref, token_ref, buffer, sems):
        total_copy = pltpu.make_async_copy(total_ref, total_out_ref, sems.at[pieces])
        total_copy.start()
        token_ref[...] = jnp.zeros_like(token_ref)
        copies = []
        for piece in range(pieces):
            part = pl.ds(piece * size, size)
            buffer[part] = lax.dot_general(
                centered_ref[:, part], code_grad_ref[...], CONTRACT_FIRST, preferred_element_type=jnp.float32
            ).astype(jnp.bfloat16)
            copies.append(pltpu.make_async_copy(buffer.at[part], grad_ref.at[part], sems.at[piece]))
            copies[-1].start()
        for copy in copies:
            copy.wait()
        total_copy.wait()

    return pl.pallas_call(
        kernel,
        out_shape=[
            jax.ShapeDtypeStruct((width, latents), jnp.bfloat16),
            jax.ShapeDtypeStruct(total.shape, jnp.float32),
            vmem(*TOKEN),
        ],
        in_specs=[VMEM] * 4,
        out_specs=[HBM, HBM, VMEM],
        scratch_shapes=[pltpu.VMEM((width, latents), jnp.bfloat16), pltpu.SemaphoreType.DMA((pieces + 1,))],
        compiler_params=pltpu.CompilerParams(vmem_limit_bytes=LIMIT),
        cost_estimate=pl.CostEstimate(flops=2 * rows * latents * width, bytes_accessed=4 * latents * width, transcendentals=0),
        name="enc_gradient",
    )(*[in_vmem(a) for a in (centered, code_grad, total, after)])


def add(terms, other, after=()):
    def kernel(terms_ref, other_ref, sum_ref):
        sum_ref[...] = terms_ref[...] + other_ref[...]

    return run(kernel, "add", [(terms.shape, jnp.float32)], [terms, other], after)[0]


def finish(terms, other, width):
    def kernel(terms_ref, other_ref, bias_ref, loss_ref):
        total = terms_ref[...] + other_ref[...]
        bias_ref[...] = total[:, :width]
        loss_ref[...] = total[:, width : width + 1] / width

    return pl.pallas_call(
        kernel,
        out_shape=[jax.ShapeDtypeStruct((1, width), jnp.float32), jax.ShapeDtypeStruct((1, 1), jnp.float32)],
        in_specs=[VMEM] * 2,
        out_specs=[VMEM] * 2,
        compiler_params=pltpu.CompilerParams(vmem_limit_bytes=2 << 20),
        name="finish",
    )(in_vmem(terms), in_vmem(other))


def local(residuals, enc_weight, enc_bias, dec_weight, dec_bias):
    own_rows, width = residuals.shape
    lat = lax.axis_size("lat")
    row_count = own_rows * lat * lax.axis_size("sub")
    far, steps = plan(lat)

    enc_vmem, own, dec_bias_row, enc_bias_row = load(
        [enc_weight, residuals, dec_bias.reshape(1, width), enc_bias.reshape(1, -1)]
    )
    paired = stack([own, swap(residuals, far)], after=[enc_vmem])
    (dec_vmem,) = load([dec_weight], after=[paired])
    rows_a = gather(paired, steps, after=[dec_vmem])
    rows_b = swap(rows_a, CORES)
    centered, active, codes_bf, keep, send, code_sum = encode_decode(
        rows_a, rows_b, enc_vmem, enc_bias_row, dec_vmem, dec_bias_row
    )

    summed = halve(keep, [swap(send, CORES)], steps[::-1])
    recon, resid_bf, own_bias, square = residual_gradient(
        summed, swap(summed, far), paired, dec_bias_row, row_count
    )

    resid_a = gather(resid_bf, steps)
    resid_b = swap(resid_a, CORES)
    code_grad_bf, total = backward(resid_a, resid_b, dec_vmem, active, row_count)
    terms = bias_product(total, enc_vmem, own_bias, square, code_sum, row_count)

    bits = [1 << b for b in range(lat.bit_length() - 1)]
    terms = add(terms, swap(terms, CORES))
    grad_enc, grad_enc_bias, enc_done = enc_gradient(centered, code_grad_bf, total, after=terms)
    for mask in bits[:-2]:
        terms = add(terms, swap(terms, mask), after=[enc_done])
    grad_dec, recon_out, dec_done = dec_gradient(codes_bf, resid_a, resid_b, recon, after=terms)
    terms = add(terms, swap(terms, bits[-2]), after=[dec_done])
    grad_dec_bias, loss_value = finish(terms, swap(terms, bits[-1]), width)
    return recon_out, loss_value[0], grad_enc, grad_enc_bias[0], grad_dec, grad_dec_bias[0]


def solution(mesh):
    placed = (
        P(("parts", "lat", "sub"), None),
        P(None, ("parts", "lat", "sub")),
        P(("parts", "lat", "sub")),
        P(("parts", "lat", "sub"), None),
        P("parts"),
    )
    return jax.shard_map(
        local,
        mesh=mesh,
        in_specs=placed,
        out_specs=(
            P(("parts", "lat", "sub"), None),
            P("parts"),
            P(None, ("parts", "lat", "sub")),
            P(("parts", "lat", "sub")),
            P(("parts", "lat", "sub"), None),
            P("parts"),
        ),
        check_vma=False,
    )
```

```python
import jax
import jax.numpy as jnp
from jax import lax
from jax.experimental import pallas as pl
from jax.experimental.pallas import tpu as pltpu
from jax.sharding import PartitionSpec as P

PENALTY = 0.2
CORES = 0
LANES = 128
LIMIT = 12 << 20
VMEM = pl.BlockSpec(memory_space=pltpu.VMEM)
HBM = pl.BlockSpec(memory_space=pltpu.HBM)
CONTRACT_FIRST = (((0,), (0,)), ((), ()))


def vmem(shape, dtype):
    return pltpu.VMEM(shape, dtype)


def in_vmem(array):
    return pltpu.with_memory_space_constraint(array, pltpu.VMEM)


def in_hbm(array):
    return pltpu.with_memory_space_constraint(array, pltpu.HBM)


TOKEN = ((8, LANES), jnp.float32)


def run(kernel, name, outs, args, after=(), flops=0, moved=0, limit=LIMIT):
    count = len(args)

    def body(*refs):
        kernel(*refs[:count], *refs[count + len(after) :])

    return pl.pallas_call(
        body,
        out_shape=[vmem(*out) for out in outs],
        in_specs=[VMEM] * (count + len(after)),
        out_specs=[VMEM] * len(outs),
        compiler_params=pltpu.CompilerParams(vmem_limit_bytes=limit),
        cost_estimate=pl.CostEstimate(flops=flops, bytes_accessed=moved, transcendentals=0),
        name=name,
    )(*[in_vmem(a) for a in args], *[in_vmem(a) for a in after])


def swap(values, mask):
    if mask == CORES:
        return lax.ppermute(values, "sub", [(i, i ^ 1) for i in range(2)])
    return lax.ppermute(values, "lat", [(i, i ^ mask) for i in range(lax.axis_size("lat"))])


ROWS_ORDER, SUM_ORDER, RESID_ORDER, TERMS_ORDER = (3, 1, 2), (2, 1, 3), (3, 1, 2), (3, 1, 2)


def plan(lat):
    bits = [1 << b for b in range(lat.bit_length() - 1)]
    near = bits[:-1]
    steps = [[1, 2, 3]] + [[b] for b in near[2:]] if len(near) > 1 else [[b] for b in near]
    return bits[-1], steps


def load(arrays, after=()):
    count = len(arrays)

    def kernel(*refs):
        copies = [
            pltpu.make_async_copy(refs[i], refs[count + len(after) + i], refs[-1].at[i]) for i in range(count)
        ]
        for copy in copies:
            copy.start()
        for copy in copies:
            copy.wait()

    return pl.pallas_call(
        kernel,
        out_shape=[vmem(array.shape, array.dtype) for array in arrays],
        in_specs=[HBM] * count + [VMEM] * len(after),
        out_specs=[VMEM] * count,
        scratch_shapes=[pltpu.SemaphoreType.DMA((count,))],
        compiler_params=pltpu.CompilerParams(vmem_limit_bytes=LIMIT),
        cost_estimate=pl.CostEstimate(
            flops=0, bytes_accessed=2 * sum(a.size * a.dtype.itemsize for a in arrays), transcendentals=0
        ),
        name="load",
    )(*[in_hbm(a) for a in arrays], *[in_vmem(a) for a in after])


def stack(blocks, after=(), order=None):
    width = blocks[0].shape[1]
    order = order or list(range(len(blocks)))

    def kernel(*refs):
        refs[-1][...] = jnp.concatenate([refs[order.index(i)][...] for i in range(len(blocks))], axis=0)

    shape = (sum(block.shape[0] for block in blocks), width)
    return run(kernel, "stack", [(shape, blocks[0].dtype)], [blocks[i] for i in order], after)[0]


def gather(rows, steps, order, after=()):
    for masks in steps:
        rows = stack([rows] + [swap(rows, mask) for mask in masks], after, [0, *order] if len(masks) > 1 else None)
    return rows


def add_parts(first, others, count, after=()):
    rows, width = first.shape
    size = rows // count

    def kernel(*refs):
        total = refs[0][...]
        for ref in refs[1 : 1 + len(others)]:
            total = total + ref[...]
        for part, ref in enumerate(refs[1 + len(others) :]):
            ref[...] = total[part * size : (part + 1) * size]

    return run(kernel, "add_parts", [((size, width), jnp.float32)] * count, [first, *others], after)


def halve(first, others, steps, dec_weight):
    for masks in steps:
        parts = add_parts(first, others, len(masks) + 1)
        dec_turned = turn(dec_weight, [parts[0]])
        first, others = parts[0], [swap(part, mask) for part, mask in zip(parts[1:], masks)]
        if len(masks) > 1:
            others = [others[mask - 1] for mask in SUM_ORDER]
    return add_parts(first, others, 1, after=[dec_turned])[0], dec_turned


def encode_rows(rows, weight, bias, dec_bias):
    centered = (rows.astype(jnp.float32) - dec_bias).astype(jnp.bfloat16)
    preact = jnp.dot(centered, weight, preferred_element_type=jnp.float32) + bias
    active = jnp.maximum(preact, 0.0)
    return centered, active, (active * active).astype(jnp.bfloat16)


def encoded(half, width, latents):
    return [((half, width), jnp.bfloat16), ((half, latents), jnp.float32), ((half, latents), jnp.bfloat16)]


def encode(rows, enc_weight, enc_bias, dec_bias):
    half, width = rows.shape
    latents = enc_weight.shape[1]

    def kernel(rows_ref, enc_ref, enc_bias_ref, dec_bias_ref, *outs):
        for ref, values in zip(outs, encode_rows(rows_ref[...], enc_ref[...], enc_bias_ref[...], dec_bias_ref[...])):
            ref[...] = values

    return run(
        kernel,
        "encode",
        encoded(half, width, latents),
        [rows, enc_weight, enc_bias, dec_bias],
        flops=2 * half * width * latents,
    )


def encode_decode(rows, codes, enc_weight, enc_bias, dec_weight, dec_bias):
    half, width = rows.shape
    latents = enc_weight.shape[1]

    def kernel(rows_ref, codes_ref, enc_ref, enc_bias_ref, dec_ref, dec_bias_ref, *outs):
        results = encode_rows(rows_ref[...], enc_ref[...], enc_bias_ref[...], dec_bias_ref[...])
        both = jnp.concatenate([codes_ref[...], results[2]], axis=0)
        partial = jnp.dot(both, dec_ref[...], preferred_element_type=jnp.float32)
        for ref, values in zip(outs, [*results, partial[:half], partial[half:]]):
            ref[...] = values

    return run(
        kernel,
        "encode_decode",
        encoded(half, width, latents) + [((half, width), jnp.float32)] * 2,
        [rows, codes, enc_weight, enc_bias, dec_weight, dec_bias],
    )


def code_sum(active_a, active_b):
    def kernel(a_ref, b_ref, sum_ref):
        total = jnp.sum(a_ref[...] * a_ref[...] + b_ref[...] * b_ref[...], keepdims=True)
        sum_ref[...] = jnp.broadcast_to(total, (1, LANES))

    return run(kernel, "code_sum", [((1, LANES), jnp.float32)], [active_a, active_b])[0]


def errors(summed_ref, other_ref, paired_ref, bias_ref):
    own = summed_ref.shape[0] // 2
    total = summed_ref[...] + jnp.concatenate([other_ref[own:], other_ref[:own]], axis=0)
    recon = total + bias_ref[...]
    return recon, recon - paired_ref[...].astype(jnp.float32)


def residual_gradient(summed, other, paired, dec_bias, row_count, after):
    def kernel(summed_ref, other_ref, paired_ref, bias_ref, resid_ref):
        _, error = errors(summed_ref, other_ref, paired_ref, bias_ref)
        resid_ref[...] = (2.0 / row_count * error).astype(jnp.bfloat16)

    return run(
        kernel, "residual_gradient", [(summed.shape, jnp.bfloat16)], [summed, other, paired, dec_bias], after
    )[0]


def own_terms(summed, other, paired, dec_bias, row_count, after):
    rows, width = summed.shape
    own = rows // 2

    def kernel(summed_ref, other_ref, paired_ref, bias_ref, recon_ref, own_ref, square_ref):
        recon, error = errors(summed_ref, other_ref, paired_ref, bias_ref)
        error = error[:own]
        recon_ref[...] = recon[:own].astype(jnp.bfloat16)
        own_ref[...] = jnp.sum(2.0 / row_count * error, axis=0, keepdims=True)
        square_ref[...] = jnp.broadcast_to(jnp.sum(error * error, keepdims=True), (1, LANES))

    return run(
        kernel,
        "own_terms",
        [((own, width), jnp.bfloat16), ((1, width), jnp.float32), ((1, LANES), jnp.float32)],
        [summed, other, paired, dec_bias],
        after,
    )


def turn(weight, after):
    rows, columns = weight.shape

    def kernel(weight_ref, turned_ref):
        turned_ref[...] = weight_ref[...].T

    return run(kernel, "turn", [((columns, rows), weight.dtype)], [weight], after, moved=4 * rows * columns)[0]


def backward(half_a, half_b, dec_weight, active_a, active_b, row_count):
    half, width = half_a.shape
    latents = dec_weight.shape[1]

    def kernel(a_ref, b_ref, dec_ref, active_a_ref, active_b_ref, code_grad_ref, total_ref):
        resid = jnp.concatenate([a_ref[...], b_ref[...]], axis=0)
        back = jnp.dot(resid, dec_ref[...], preferred_element_type=jnp.float32)
        active = jnp.concatenate([active_a_ref[...], active_b_ref[...]], axis=0)
        code_grad = 2.0 * active * (back + PENALTY / row_count)
        code_grad_ref[...] = code_grad.astype(jnp.bfloat16)
        total_ref[...] = jnp.sum(code_grad, axis=0, keepdims=True)

    return run(
        kernel,
        "backward",
        [((2 * half, latents), jnp.bfloat16), ((1, latents), jnp.float32)],
        [half_a, half_b, dec_weight, active_a, active_b],
    )


def bias_product(total, enc_weight, own_bias, square, code_sum, row_count):
    latents, width = enc_weight.shape

    def kernel(total_ref, enc_ref, own_ref, square_ref, sum_ref, terms_ref):
        values = total_ref[...]
        high = values.astype(jnp.bfloat16).astype(jnp.float32)
        rest = values - high
        middle = rest.astype(jnp.bfloat16).astype(jnp.float32)
        pieces = [high, middle, rest - middle, jnp.zeros((5, latents), jnp.float32)]
        pieces = jnp.concatenate(pieces, axis=0).astype(jnp.bfloat16)
        product = jnp.dot(pieces, enc_ref[...], preferred_element_type=jnp.float32)
        terms_ref[:, :width] = own_ref[...] - (product[0:1] + (product[1:2] + product[2:3]))
        terms_ref[:, width:] = (square_ref[...] + PENALTY * sum_ref[...]) / row_count

    return run(
        kernel,
        "bias_product",
        [((1, width + LANES), jnp.float32)],
        [total, enc_weight, own_bias, square, code_sum],
    )[0]


def enc_gradient(centered_a, centered_b, code_grad, after):
    half, width = centered_a.shape
    latents = code_grad.shape[1]

    def kernel(a_ref, b_ref, code_grad_ref, grad_ref):
        centered = jnp.concatenate([a_ref[...], b_ref[...]], axis=0)
        grad_ref[...] = lax.dot_general(
            centered, code_grad_ref[...], CONTRACT_FIRST, preferred_element_type=jnp.float32
        ).astype(jnp.bfloat16)

    return run(
        kernel,
        "enc_gradient",
        [((width, latents), jnp.bfloat16)],
        [centered_a, centered_b, code_grad],
        after,
        flops=4 * half * width * latents,
    )[0]


def dec_gradient(codes_a, codes_b, resid_a, resid_b, stored, after):
    half, latents = codes_a.shape
    width = resid_a.shape[1]
    count = len(stored)

    def kernel(*refs):
        codes_a_ref, codes_b_ref, a_ref, b_ref = refs[:4]
        outs, grad_ref, sems = refs[5 + count : 5 + 2 * count], refs[-2], refs[-1]
        copies = [pltpu.make_async_copy(refs[4 + i], outs[i], sems.at[i]) for i in range(count)]
        for copy in copies:
            copy.start()
        codes = jnp.concatenate([codes_a_ref[...], codes_b_ref[...]], axis=0)
        resid = jnp.concatenate([a_ref[...], b_ref[...]], axis=0)
        grad_ref[...] = lax.dot_general(
            codes, resid, CONTRACT_FIRST, preferred_element_type=jnp.float32
        ).astype(jnp.bfloat16)
        for copy in copies:
            copy.wait()

    *outs, grad = pl.pallas_call(
        kernel,
        out_shape=[jax.ShapeDtypeStruct(a.shape, a.dtype) for a in stored] + [vmem((latents, width), jnp.bfloat16)],
        in_specs=[VMEM] * (5 + count),
        out_specs=[HBM] * count + [VMEM],
        scratch_shapes=[pltpu.SemaphoreType.DMA((count,))],
        compiler_params=pltpu.CompilerParams(vmem_limit_bytes=LIMIT),
        cost_estimate=pl.CostEstimate(flops=4 * half * latents * width, bytes_accessed=4 * latents * width, transcendentals=0),
        name="dec_gradient",
    )(*[in_vmem(a) for a in (codes_a, codes_b, resid_a, resid_b, *stored, after)])
    return outs, grad


def store(arrays, after):
    count = len(arrays)

    def kernel(*refs):
        outs, token_ref, sems = refs[count + 1 : 2 * count + 1], refs[-2], refs[-1]
        copies = [pltpu.make_async_copy(refs[i], outs[i], sems.at[i]) for i in range(count)]
        for copy in copies:
            copy.start()
        token_ref[...] = jnp.zeros_like(token_ref)
        for copy in copies:
            copy.wait()

    return pl.pallas_call(
        kernel,
        out_shape=[jax.ShapeDtypeStruct(a.shape, a.dtype) for a in arrays] + [vmem(*TOKEN)],
        in_specs=[VMEM] * (count + 1),
        out_specs=[HBM] * count + [VMEM],
        scratch_shapes=[pltpu.SemaphoreType.DMA((count,))],
        compiler_params=pltpu.CompilerParams(vmem_limit_bytes=LIMIT),
        cost_estimate=pl.CostEstimate(
            flops=0, bytes_accessed=2 * sum(a.size * a.dtype.itemsize for a in arrays), transcendentals=0
        ),
        name="store",
    )(*[in_vmem(a) for a in (*arrays, after)])


def add(*terms, after=(), order=None):
    order = order or list(range(len(terms)))

    def kernel(*refs):
        values = [refs[order.index(i)][...] for i in range(len(terms))]
        while len(values) > 1:
            values = [left + right for left, right in zip(values[::2], values[1::2])]
        refs[-1][...] = values[0]

    return run(kernel, "add", [(terms[0].shape, jnp.float32)], [terms[i] for i in order], after)[0]


def finish(terms, other, width, after):
    def kernel(terms_ref, other_ref, after_ref, bias_ref, loss_ref):
        total = terms_ref[...] + other_ref[...]
        bias_ref[...] = total[:, :width]
        loss_ref[...] = total[:, width : width + 1] / width

    return pl.pallas_call(
        kernel,
        out_shape=[jax.ShapeDtypeStruct((1, width), jnp.float32), jax.ShapeDtypeStruct((1, 1), jnp.float32)],
        in_specs=[VMEM] * 3,
        out_specs=[VMEM] * 2,
        compiler_params=pltpu.CompilerParams(vmem_limit_bytes=2 << 20),
        name="finish",
    )(in_vmem(terms), in_vmem(other), in_vmem(after))


def local(residuals, enc_weight, enc_bias, dec_weight, dec_bias):
    own_rows, width = residuals.shape
    lat = lax.axis_size("lat")
    row_count = own_rows * lat * lax.axis_size("sub")
    far, steps = plan(lat)

    enc_vmem, own, dec_bias_row, enc_bias_row = load(
        [enc_weight, residuals, dec_bias.reshape(1, width), enc_bias.reshape(1, -1)]
    )
    paired = stack([own, swap(residuals, far)], after=[enc_vmem])
    (dec_vmem,) = load([dec_weight], after=[paired])
    rows_a = gather(paired, steps, ROWS_ORDER, after=[dec_vmem])
    rows_b = swap(rows_a, CORES)
    centered_a, active_a, codes_a = encode(rows_a, enc_vmem, enc_bias_row, dec_bias_row)
    centered_b, active_b, codes_b, keep, send = encode_decode(
        rows_b, codes_a, enc_vmem, enc_bias_row, dec_vmem, dec_bias_row
    )

    summed, dec_turned = halve(keep, [swap(send, CORES)], steps[::-1], dec_vmem)
    enc_turned = turn(enc_vmem, [summed])
    error_args = summed, swap(summed, far), paired, dec_bias_row, row_count
    resid_bf = residual_gradient(*error_args, [enc_turned])

    resid_a = gather(resid_bf, steps, RESID_ORDER)
    resid_b = swap(resid_a, CORES)
    recon, own_bias, square = own_terms(*error_args, [resid_bf])
    code_grad_bf, total = backward(resid_a, resid_b, dec_turned, active_a, active_b, row_count)
    terms = bias_product(total, enc_turned, own_bias, square, code_sum(active_a, active_b), row_count)

    grad_enc = enc_gradient(centered_a, centered_b, code_grad_bf, [terms])
    terms = add(terms, swap(terms, CORES), after=[grad_enc])
    (grad_enc, total), grad_dec = dec_gradient(codes_a, codes_b, resid_a, resid_b, [grad_enc, total], terms)
    for masks in steps:
        terms = add(
            terms,
            *[swap(terms, mask) for mask in masks],
            after=[grad_dec],
            order=[0, *TERMS_ORDER] if len(masks) > 1 else None,
        )
    grad_dec, recon, stored = store([grad_dec, recon], terms)
    grad_dec_bias, loss_value = finish(terms, swap(terms, far), width, stored)
    return recon, loss_value[0], grad_enc, total[0], grad_dec, grad_dec_bias[0]


def solution(mesh):
    placed = (
        P(("parts", "lat", "sub"), None),
        P(None, ("parts", "lat", "sub")),
        P(("parts", "lat", "sub")),
        P(("parts", "lat", "sub"), None),
        P("parts"),
    )
    return jax.shard_map(
        local,
        mesh=mesh,
        in_specs=placed,
        out_specs=(
            P(("parts", "lat", "sub"), None),
            P("parts"),
            P(None, ("parts", "lat", "sub")),
            P(("parts", "lat", "sub")),
            P(("parts", "lat", "sub"), None),
            P("parts"),
        ),
        check_vma=False,
    )
```

```python
import jax
import jax.numpy as jnp
from jax import lax
from jax.experimental import pallas as pl
from jax.experimental.pallas import tpu as pltpu
from jax.sharding import PartitionSpec as P

PENALTY = 0.2
CORES = 0
LANES = 128
LIMIT = 12 << 20
VMEM = pl.BlockSpec(memory_space=pltpu.VMEM)
HBM = pl.BlockSpec(memory_space=pltpu.HBM)
CONTRACT_FIRST = (((0,), (0,)), ((), ()))


def vmem(shape, dtype):
    return pltpu.VMEM(shape, dtype)


def in_vmem(array):
    return pltpu.with_memory_space_constraint(array, pltpu.VMEM)


def in_hbm(array):
    return pltpu.with_memory_space_constraint(array, pltpu.HBM)


TOKEN = ((8, LANES), jnp.float32)


def run(kernel, name, outs, args, after=(), flops=0, moved=0, limit=LIMIT):
    count = len(args)

    def body(*refs):
        kernel(*refs[:count], *refs[count + len(after) :])

    return pl.pallas_call(
        body,
        out_shape=[vmem(*out) for out in outs],
        in_specs=[VMEM] * (count + len(after)),
        out_specs=[VMEM] * len(outs),
        compiler_params=pltpu.CompilerParams(vmem_limit_bytes=limit),
        cost_estimate=pl.CostEstimate(flops=flops, bytes_accessed=moved, transcendentals=0),
        name=name,
    )(*[in_vmem(a) for a in args], *[in_vmem(a) for a in after])


def swap(values, mask):
    if mask == CORES:
        return lax.ppermute(values, "sub", [(i, i ^ 1) for i in range(2)])
    return lax.ppermute(values, "lat", [(i, i ^ mask) for i in range(lax.axis_size("lat"))])


ROWS_ORDER, SUM_ORDER, RESID_ORDER, TERMS_ORDER = (2, 1, 3), (2, 1, 3), (2, 1, 3), (2, 1, 3)


def plan(lat):
    bits = [1 << b for b in range(lat.bit_length() - 1)]
    near = bits[:-1]
    steps = [[1, 2, 3]] + [[b] for b in near[2:]] if len(near) > 1 else [[b] for b in near]
    return bits[-1], steps


def load(arrays, after=()):
    count = len(arrays)

    def kernel(*refs):
        copies = [
            pltpu.make_async_copy(refs[i], refs[count + len(after) + i], refs[-1].at[i]) for i in range(count)
        ]
        for copy in copies:
            copy.start()
        for copy in copies:
            copy.wait()

    return pl.pallas_call(
        kernel,
        out_shape=[vmem(array.shape, array.dtype) for array in arrays],
        in_specs=[HBM] * count + [VMEM] * len(after),
        out_specs=[VMEM] * count,
        scratch_shapes=[pltpu.SemaphoreType.DMA((count,))],
        compiler_params=pltpu.CompilerParams(vmem_limit_bytes=LIMIT),
        cost_estimate=pl.CostEstimate(
            flops=0, bytes_accessed=2 * sum(a.size * a.dtype.itemsize for a in arrays), transcendentals=0
        ),
        name="load",
    )(*[in_hbm(a) for a in arrays], *[in_vmem(a) for a in after])


def stack(blocks, after=(), order=None):
    width = blocks[0].shape[1]
    order = order or list(range(len(blocks)))

    def kernel(*refs):
        refs[-1][...] = jnp.concatenate([refs[order.index(i)][...] for i in range(len(blocks))], axis=0)

    shape = (sum(block.shape[0] for block in blocks), width)
    return run(kernel, "stack", [(shape, blocks[0].dtype)], [blocks[i] for i in order], after)[0]


def gather(rows, steps, order, after=()):
    for masks in steps:
        rows = stack([rows] + [swap(rows, mask) for mask in masks], after, [0, *order] if len(masks) > 1 else None)
    return rows


def add_parts(first, others, count, after=()):
    rows, width = first.shape
    size = rows // count

    def kernel(*refs):
        total = refs[0][...]
        for ref in refs[1 : 1 + len(others)]:
            total = total + ref[...]
        for part, ref in enumerate(refs[1 + len(others) :]):
            ref[...] = total[part * size : (part + 1) * size]

    return run(kernel, "add_parts", [((size, width), jnp.float32)] * count, [first, *others], after)


def halve(parts, steps, dec_weight):
    dec_turned = turn(dec_weight, [parts[0]])
    for step, masks in enumerate(steps):
        others = [swap(part, mask) for part, mask in zip(parts[1:], masks)]
        if len(masks) > 1:
            others = [others[mask - 1] for mask in SUM_ORDER]
        count = len(steps[step + 1]) + 1 if step + 1 < len(steps) else 1
        parts = add_parts(parts[0], others, count, after=[dec_turned])
    return parts[0], dec_turned


def encode_decode(rows, weights, dec_bias, count):
    height, width = rows.shape
    latents = weights[0][0].shape[1]
    sets = len(weights)

    def kernel(rows_ref, dec_bias_ref, *refs):
        centered_ref, outs = refs[3 * sets], refs[3 * sets + 1 :]
        centered = (rows_ref[...].astype(jnp.float32) - dec_bias_ref[...]).astype(jnp.bfloat16)
        centered_ref[...] = centered
        codes = []
        for i in range(sets):
            enc_ref, enc_bias_ref = refs[3 * i], refs[3 * i + 1]
            preact = jnp.dot(centered, enc_ref[...], preferred_element_type=jnp.float32) + enc_bias_ref[...]
            active = jnp.maximum(preact, 0.0)
            outs[i][...] = active
            codes.append((active * active).astype(jnp.bfloat16))
        total = None
        for i in range(sets):
            partial = jnp.dot(codes[i], refs[3 * i + 2][...], preferred_element_type=jnp.float32)
            total = partial if total is None else total + partial
        size = height // count
        for part, ref in enumerate(outs[sets:]):
            ref[...] = total[part * size : (part + 1) * size]

    return run(
        kernel,
        "encode_decode",
        [((height, width), jnp.bfloat16)]
        + [((height, latents), jnp.float32)] * sets
        + [((height // count, width), jnp.float32)] * count,
        [rows, dec_bias, *[array for weight in weights for array in weight]],
        flops=4 * sets * height * width * latents,
    )


def code_sum(active_a, active_b):
    def kernel(a_ref, b_ref, sum_ref):
        total = jnp.sum(a_ref[...] * a_ref[...] + b_ref[...] * b_ref[...], keepdims=True)
        sum_ref[...] = jnp.broadcast_to(total, (1, LANES))

    return run(kernel, "code_sum", [((1, LANES), jnp.float32)], [active_a, active_b])[0]


def errors(summed_ref, other_ref, paired_ref, bias_ref):
    own = summed_ref.shape[0] // 2
    total = summed_ref[...] + jnp.concatenate([other_ref[own:], other_ref[:own]], axis=0)
    recon = total + bias_ref[...]
    return recon, recon - paired_ref[...].astype(jnp.float32)


def residual_gradient(summed, other, paired, dec_bias, row_count, after):
    def kernel(summed_ref, other_ref, paired_ref, bias_ref, resid_ref):
        _, error = errors(summed_ref, other_ref, paired_ref, bias_ref)
        resid_ref[...] = (2.0 / row_count * error).astype(jnp.bfloat16)

    return run(
        kernel, "residual_gradient", [(summed.shape, jnp.bfloat16)], [summed, other, paired, dec_bias], after
    )[0]


def own_terms(summed, other, paired, dec_bias, row_count, after):
    rows, width = summed.shape
    own = rows // 2

    def kernel(summed_ref, other_ref, paired_ref, bias_ref, recon_ref, own_ref, square_ref):
        recon, error = errors(summed_ref, other_ref, paired_ref, bias_ref)
        error = error[:own]
        recon_ref[...] = recon[:own].astype(jnp.bfloat16)
        own_ref[...] = jnp.sum(2.0 / row_count * error, axis=0, keepdims=True)
        square_ref[...] = jnp.broadcast_to(jnp.sum(error * error, keepdims=True), (1, LANES))

    return run(
        kernel,
        "own_terms",
        [((own, width), jnp.bfloat16), ((1, width), jnp.float32), ((1, LANES), jnp.float32)],
        [summed, other, paired, dec_bias],
        after,
    )


def turn(weight, after):
    rows, columns = weight.shape

    def kernel(weight_ref, turned_ref):
        turned_ref[...] = weight_ref[...].T

    return run(kernel, "turn", [((columns, rows), weight.dtype)], [weight], after, moved=4 * rows * columns)[0]


def backward(half_a, half_b, dec_weight, active_a, active_b, row_count):
    half, width = half_a.shape
    latents = dec_weight.shape[1]

    def kernel(a_ref, b_ref, dec_ref, active_a_ref, active_b_ref, code_grad_ref, total_ref):
        resid = jnp.concatenate([a_ref[...], b_ref[...]], axis=0)
        back = jnp.dot(resid, dec_ref[...], preferred_element_type=jnp.float32)
        active = jnp.concatenate([active_a_ref[...], active_b_ref[...]], axis=0)
        code_grad = 2.0 * active * (back + PENALTY / row_count)
        code_grad_ref[...] = code_grad.astype(jnp.bfloat16)
        total_ref[...] = jnp.sum(code_grad, axis=0, keepdims=True)

    return run(
        kernel,
        "backward",
        [((2 * half, latents), jnp.bfloat16), ((1, latents), jnp.float32)],
        [half_a, half_b, dec_weight, active_a, active_b],
    )


def bias_product(total, enc_weight, own_bias, square, code_sum, row_count):
    latents, width = enc_weight.shape

    def kernel(total_ref, enc_ref, own_ref, square_ref, sum_ref, terms_ref):
        values = total_ref[...]
        high = values.astype(jnp.bfloat16).astype(jnp.float32)
        rest = values - high
        middle = rest.astype(jnp.bfloat16).astype(jnp.float32)
        pieces = [high, middle, rest - middle, jnp.zeros((5, latents), jnp.float32)]
        pieces = jnp.concatenate(pieces, axis=0).astype(jnp.bfloat16)
        product = jnp.dot(pieces, enc_ref[...], preferred_element_type=jnp.float32)
        terms_ref[:, :width] = own_ref[...] - (product[0:1] + (product[1:2] + product[2:3]))
        terms_ref[:, width:] = (square_ref[...] + PENALTY * sum_ref[...]) / row_count

    return run(
        kernel,
        "bias_product",
        [((1, width + LANES), jnp.float32)],
        [total, enc_weight, own_bias, square, code_sum],
    )[0]


def enc_gradient(centered_a, centered_b, code_grad, after):
    half, width = centered_a.shape
    latents = code_grad.shape[1]

    def kernel(a_ref, b_ref, code_grad_ref, grad_ref):
        centered = jnp.concatenate([a_ref[...], b_ref[...]], axis=0)
        grad_ref[...] = lax.dot_general(
            centered, code_grad_ref[...], CONTRACT_FIRST, preferred_element_type=jnp.float32
        ).astype(jnp.bfloat16)

    return run(
        kernel,
        "enc_gradient",
        [((width, latents), jnp.bfloat16)],
        [centered_a, centered_b, code_grad],
        after,
        flops=4 * half * width * latents,
    )[0]


def dec_gradient(active_a, active_b, resid_a, resid_b, stored, after):
    half, latents = active_a.shape
    width = resid_a.shape[1]
    count = len(stored)

    def kernel(*refs):
        active_a_ref, active_b_ref, a_ref, b_ref = refs[:4]
        outs, grad_ref, sems = refs[5 + count : 5 + 2 * count], refs[-2], refs[-1]
        copies = [pltpu.make_async_copy(refs[4 + i], outs[i], sems.at[i]) for i in range(count)]
        for copy in copies:
            copy.start()
        active = jnp.concatenate([active_a_ref[...], active_b_ref[...]], axis=0)
        codes = (active * active).astype(jnp.bfloat16)
        resid = jnp.concatenate([a_ref[...], b_ref[...]], axis=0)
        grad_ref[...] = lax.dot_general(
            codes, resid, CONTRACT_FIRST, preferred_element_type=jnp.float32
        ).astype(jnp.bfloat16)
        for copy in copies:
            copy.wait()

    *outs, grad = pl.pallas_call(
        kernel,
        out_shape=[jax.ShapeDtypeStruct(a.shape, a.dtype) for a in stored] + [vmem((latents, width), jnp.bfloat16)],
        in_specs=[VMEM] * (5 + count),
        out_specs=[HBM] * count + [VMEM],
        scratch_shapes=[pltpu.SemaphoreType.DMA((count,))],
        compiler_params=pltpu.CompilerParams(vmem_limit_bytes=LIMIT),
        cost_estimate=pl.CostEstimate(flops=4 * half * latents * width, bytes_accessed=4 * latents * width, transcendentals=0),
        name="dec_gradient",
    )(*[in_vmem(a) for a in (active_a, active_b, resid_a, resid_b, *stored, after)])
    return outs, grad


def store(arrays, after):
    count = len(arrays)

    def kernel(*refs):
        outs, token_ref, sems = refs[count + 1 : 2 * count + 1], refs[-2], refs[-1]
        copies = [pltpu.make_async_copy(refs[i], outs[i], sems.at[i]) for i in range(count)]
        for copy in copies:
            copy.start()
        token_ref[...] = jnp.zeros_like(token_ref)
        for copy in copies:
            copy.wait()

    return pl.pallas_call(
        kernel,
        out_shape=[jax.ShapeDtypeStruct(a.shape, a.dtype) for a in arrays] + [vmem(*TOKEN)],
        in_specs=[VMEM] * (count + 1),
        out_specs=[HBM] * count + [VMEM],
        scratch_shapes=[pltpu.SemaphoreType.DMA((count,))],
        compiler_params=pltpu.CompilerParams(vmem_limit_bytes=LIMIT),
        cost_estimate=pl.CostEstimate(
            flops=0, bytes_accessed=2 * sum(a.size * a.dtype.itemsize for a in arrays), transcendentals=0
        ),
        name="store",
    )(*[in_vmem(a) for a in (*arrays, after)])


def add(*terms, after=(), order=None):
    order = order or list(range(len(terms)))

    def kernel(*refs):
        values = [refs[order.index(i)][...] for i in range(len(terms))]
        while len(values) > 1:
            values = [left + right for left, right in zip(values[::2], values[1::2])]
        refs[-1][...] = values[0]

    return run(kernel, "add", [(terms[0].shape, jnp.float32)], [terms[i] for i in order], after)[0]


def finish(terms, other, width, after):
    def kernel(terms_ref, other_ref, after_ref, bias_ref, loss_ref):
        total = terms_ref[...] + other_ref[...]
        bias_ref[...] = total[:, :width]
        loss_ref[...] = total[:, width : width + 1] / width

    return pl.pallas_call(
        kernel,
        out_shape=[jax.ShapeDtypeStruct((1, width), jnp.float32), jax.ShapeDtypeStruct((1, 1), jnp.float32)],
        in_specs=[VMEM] * 3,
        out_specs=[VMEM] * 2,
        compiler_params=pltpu.CompilerParams(vmem_limit_bytes=2 << 20),
        name="finish",
    )(in_vmem(terms), in_vmem(other), in_vmem(after))


def local(residuals, enc_weight, enc_bias, dec_weight, dec_bias):
    own_rows, width = residuals.shape
    lat = lax.axis_size("lat")
    row_count = own_rows * lat * lax.axis_size("sub")
    far, steps = plan(lat)

    enc_bias = enc_bias.reshape(1, -1)
    other = swap(residuals, far)
    siblings = swap(enc_weight, CORES), swap(enc_bias, CORES), swap(dec_weight, CORES)
    enc_vmem, own, dec_bias_row, enc_bias_row = load([enc_weight, residuals, dec_bias.reshape(1, width), enc_bias])
    paired = stack([own, other], after=[enc_vmem])
    (dec_vmem,) = load([dec_weight], after=[paired])
    rows = gather(paired, steps, ROWS_ORDER, after=[dec_vmem])
    centered_a, active_a, active_sibling, *parts = encode_decode(
        rows, [(enc_vmem, enc_bias_row, dec_vmem), siblings], dec_bias_row, len(steps[-1]) + 1
    )

    summed, dec_turned = halve(parts, steps[::-1], dec_vmem)
    active_b = swap(active_sibling, CORES)
    centered_b = swap(centered_a, CORES)
    enc_turned = turn(enc_vmem, [summed])
    error_args = summed, swap(summed, far), paired, dec_bias_row, row_count
    resid_bf = residual_gradient(*error_args, [enc_turned, active_b, centered_b])

    resid_a = gather(resid_bf, steps, RESID_ORDER)
    resid_b = swap(resid_a, CORES)
    recon, own_bias, square = own_terms(*error_args, [resid_bf])
    code_grad_bf, total = backward(resid_a, resid_b, dec_turned, active_a, active_b, row_count)
    terms = bias_product(total, enc_turned, own_bias, square, code_sum(active_a, active_b), row_count)

    grad_enc = enc_gradient(centered_a, centered_b, code_grad_bf, [terms])
    terms = add(terms, swap(terms, CORES), after=[grad_enc])
    (grad_enc, total), grad_dec = dec_gradient(active_a, active_b, resid_a, resid_b, [grad_enc, total], terms)
    for masks in steps:
        terms = add(
            terms,
            *[swap(terms, mask) for mask in masks],
            after=[grad_dec],
            order=[0, *TERMS_ORDER] if len(masks) > 1 else None,
        )
    grad_dec, recon, stored = store([grad_dec, recon], terms)
    grad_dec_bias, loss_value = finish(terms, swap(terms, far), width, stored)
    return recon, loss_value[0], grad_enc, total[0], grad_dec, grad_dec_bias[0]


def solution(mesh):
    placed = (
        P(("parts", "lat", "sub"), None),
        P(None, ("parts", "lat", "sub")),
        P(("parts", "lat", "sub")),
        P(("parts", "lat", "sub"), None),
        P("parts"),
    )
    return jax.shard_map(
        local,
        mesh=mesh,
        in_specs=placed,
        out_specs=(
            P(("parts", "lat", "sub"), None),
            P("parts"),
            P(None, ("parts", "lat", "sub")),
            P(("parts", "lat", "sub")),
            P(("parts", "lat", "sub"), None),
            P("parts"),
        ),
        check_vma=False,
    )
```

```python
import jax
import jax.numpy as jnp
from jax import lax
from jax.experimental import pallas as pl
from jax.experimental.pallas import tpu as pltpu
from jax.sharding import PartitionSpec as P

PENALTY = 0.2
CORES = 0
LANES = 128
LIMIT = 12 << 20
VMEM = pl.BlockSpec(memory_space=pltpu.VMEM)
HBM = pl.BlockSpec(memory_space=pltpu.HBM)
CONTRACT_FIRST = (((0,), (0,)), ((), ()))


def vmem(shape, dtype):
    return pltpu.VMEM(shape, dtype)


def in_vmem(array):
    return pltpu.with_memory_space_constraint(array, pltpu.VMEM)


def in_hbm(array):
    return pltpu.with_memory_space_constraint(array, pltpu.HBM)


TOKEN = ((8, LANES), jnp.float32)


def run(kernel, name, outs, args, after=(), flops=0, moved=0, limit=LIMIT):
    count = len(args)

    def body(*refs):
        kernel(*refs[:count], *refs[count + len(after) :])

    return pl.pallas_call(
        body,
        out_shape=[vmem(*out) for out in outs],
        in_specs=[VMEM] * (count + len(after)),
        out_specs=[VMEM] * len(outs),
        compiler_params=pltpu.CompilerParams(vmem_limit_bytes=limit),
        cost_estimate=pl.CostEstimate(flops=flops, bytes_accessed=moved, transcendentals=0),
        name=name,
    )(*[in_vmem(a) for a in args], *[in_vmem(a) for a in after])


def swap(values, mask):
    if mask == CORES:
        return lax.ppermute(values, "sub", [(i, i ^ 1) for i in range(2)])
    return lax.ppermute(values, "lat", [(i, i ^ mask) for i in range(lax.axis_size("lat"))])


ROWS_ORDER, SUM_ORDER, RESID_ORDER, TERMS_ORDER = (2, 3, 1), (1, 3, 2), (2, 1, 3), (2, 3, 1)


def plan(lat):
    bits = [1 << b for b in range(lat.bit_length() - 1)]
    near = bits[:-1]
    steps = [[1, 2, 3]] + [[b] for b in near[2:]] if len(near) > 1 else [[b] for b in near]
    return bits[-1], steps


def load(arrays, after=()):
    count = len(arrays)

    def kernel(*refs):
        copies = [
            pltpu.make_async_copy(refs[i], refs[count + len(after) + i], refs[-1].at[i]) for i in range(count)
        ]
        for copy in copies:
            copy.start()
        for copy in copies:
            copy.wait()

    return pl.pallas_call(
        kernel,
        out_shape=[vmem(array.shape, array.dtype) for array in arrays],
        in_specs=[HBM] * count + [VMEM] * len(after),
        out_specs=[VMEM] * count,
        scratch_shapes=[pltpu.SemaphoreType.DMA((count,))],
        compiler_params=pltpu.CompilerParams(vmem_limit_bytes=LIMIT),
        cost_estimate=pl.CostEstimate(
            flops=0, bytes_accessed=2 * sum(a.size * a.dtype.itemsize for a in arrays), transcendentals=0
        ),
        name="load",
    )(*[in_hbm(a) for a in arrays], *[in_vmem(a) for a in after])


def stack(blocks, after=(), order=None):
    width = blocks[0].shape[1]
    order = order or list(range(len(blocks)))

    def kernel(*refs):
        refs[-1][...] = jnp.concatenate([refs[order.index(i)][...] for i in range(len(blocks))], axis=0)

    shape = (sum(block.shape[0] for block in blocks), width)
    return run(kernel, "stack", [(shape, blocks[0].dtype)], [blocks[i] for i in order], after)[0]


def gather(rows, steps, order, after=()):
    for masks in steps:
        rows = stack([rows] + [swap(rows, mask) for mask in masks], after, [0, *order] if len(masks) > 1 else None)
    return rows


def add_parts(first, others, count, after=()):
    rows, width = first.shape
    size = rows // count

    def kernel(*refs):
        total = refs[0][...]
        for ref in refs[1 : 1 + len(others)]:
            total = total + ref[...]
        for part, ref in enumerate(refs[1 + len(others) :]):
            ref[...] = total[part * size : (part + 1) * size]

    return run(kernel, "add_parts", [((size, width), jnp.float32)] * count, [first, *others], after)


def halve(parts, steps, dec_weight):
    dec_turned = turn(dec_weight, [parts[0]])
    for step, masks in enumerate(steps):
        others = [swap(part, mask) for part, mask in zip(parts[1:], masks)]
        if len(masks) > 1:
            others = [others[mask - 1] for mask in SUM_ORDER]
        count = len(steps[step + 1]) + 1 if step + 1 < len(steps) else 1
        parts = add_parts(parts[0], others, count, after=[dec_turned])
    return parts[0], dec_turned


def encode_decode(rows, weights, dec_bias, count):
    height, width = rows.shape
    latents = weights[0][0].shape[1]
    sets = len(weights)

    def kernel(rows_ref, dec_bias_ref, *refs):
        centered_ref, outs = refs[3 * sets], refs[3 * sets + 1 :]
        centered = (rows_ref[...].astype(jnp.float32) - dec_bias_ref[...]).astype(jnp.bfloat16)
        centered_ref[...] = centered
        codes = []
        for i in range(sets):
            enc_ref, enc_bias_ref = refs[3 * i], refs[3 * i + 1]
            preact = jnp.dot(centered, enc_ref[...], preferred_element_type=jnp.float32) + enc_bias_ref[...]
            active = jnp.maximum(preact, 0.0)
            outs[i][...] = active
            codes.append((active * active).astype(jnp.bfloat16))
        total = None
        for i in range(sets):
            partial = jnp.dot(codes[i], refs[3 * i + 2][...], preferred_element_type=jnp.float32)
            total = partial if total is None else total + partial
        size = height // count
        for part, ref in enumerate(outs[sets:]):
            ref[...] = total[part * size : (part + 1) * size]

    return run(
        kernel,
        "encode_decode",
        [((height, width), jnp.bfloat16)]
        + [((height, latents), jnp.float32)] * sets
        + [((height // count, width), jnp.float32)] * count,
        [rows, dec_bias, *[array for weight in weights for array in weight]],
        flops=4 * sets * height * width * latents,
    )


def code_sum(active_a, active_b):
    def kernel(a_ref, b_ref, sum_ref):
        total = jnp.sum(a_ref[...] * a_ref[...] + b_ref[...] * b_ref[...], keepdims=True)
        sum_ref[...] = jnp.broadcast_to(total, (1, LANES))

    return run(kernel, "code_sum", [((1, LANES), jnp.float32)], [active_a, active_b])[0]


def errors(summed_ref, other_ref, paired_ref, bias_ref):
    own = summed_ref.shape[0] // 2
    total = summed_ref[...] + jnp.concatenate([other_ref[own:], other_ref[:own]], axis=0)
    recon = total + bias_ref[...]
    return recon, recon - paired_ref[...].astype(jnp.float32)


def residual_gradient(summed, other, paired, dec_bias, row_count, after):
    def kernel(summed_ref, other_ref, paired_ref, bias_ref, resid_ref):
        _, error = errors(summed_ref, other_ref, paired_ref, bias_ref)
        resid_ref[...] = (2.0 / row_count * error).astype(jnp.bfloat16)

    return run(
        kernel, "residual_gradient", [(summed.shape, jnp.bfloat16)], [summed, other, paired, dec_bias], after
    )[0]


def own_terms(summed, other, paired, dec_bias, row_count, after):
    rows, width = summed.shape
    own = rows // 2

    def kernel(summed_ref, other_ref, paired_ref, bias_ref, recon_ref, own_ref, square_ref):
        recon, error = errors(summed_ref, other_ref, paired_ref, bias_ref)
        error = error[:own]
        recon_ref[...] = recon[:own].astype(jnp.bfloat16)
        own_ref[...] = jnp.sum(2.0 / row_count * error, axis=0, keepdims=True)
        square_ref[...] = jnp.broadcast_to(jnp.sum(error * error, keepdims=True), (1, LANES))

    return run(
        kernel,
        "own_terms",
        [((own, width), jnp.bfloat16), ((1, width), jnp.float32), ((1, LANES), jnp.float32)],
        [summed, other, paired, dec_bias],
        after,
    )


def turn(weight, after):
    rows, columns = weight.shape

    def kernel(weight_ref, turned_ref):
        turned_ref[...] = weight_ref[...].T

    return run(kernel, "turn", [((columns, rows), weight.dtype)], [weight], after, moved=4 * rows * columns)[0]


def backward(half_a, half_b, dec_weight, active_a, active_b, row_count):
    half, width = half_a.shape
    latents = dec_weight.shape[1]

    def kernel(a_ref, b_ref, dec_ref, active_a_ref, active_b_ref, code_grad_ref, total_ref):
        resid = jnp.concatenate([a_ref[...], b_ref[...]], axis=0)
        back = jnp.dot(resid, dec_ref[...], preferred_element_type=jnp.float32)
        active = jnp.concatenate([active_a_ref[...], active_b_ref[...]], axis=0)
        code_grad = 2.0 * active * (back + PENALTY / row_count)
        code_grad_ref[...] = code_grad.astype(jnp.bfloat16)
        total_ref[...] = jnp.sum(code_grad, axis=0, keepdims=True)

    return run(
        kernel,
        "backward",
        [((2 * half, latents), jnp.bfloat16), ((1, latents), jnp.float32)],
        [half_a, half_b, dec_weight, active_a, active_b],
    )


def bias_product(total, enc_weight, own_bias, square, code_sum, row_count):
    latents, width = enc_weight.shape

    def kernel(total_ref, enc_ref, own_ref, square_ref, sum_ref, terms_ref):
        values = total_ref[...]
        high = values.astype(jnp.bfloat16).astype(jnp.float32)
        rest = values - high
        middle = rest.astype(jnp.bfloat16).astype(jnp.float32)
        pieces = [high, middle, rest - middle, jnp.zeros((5, latents), jnp.float32)]
        pieces = jnp.concatenate(pieces, axis=0).astype(jnp.bfloat16)
        product = jnp.dot(pieces, enc_ref[...], preferred_element_type=jnp.float32)
        terms_ref[:, :width] = own_ref[...] - (product[0:1] + (product[1:2] + product[2:3]))
        terms_ref[:, width:] = (square_ref[...] + PENALTY * sum_ref[...]) / row_count

    return run(
        kernel,
        "bias_product",
        [((1, width + LANES), jnp.float32)],
        [total, enc_weight, own_bias, square, code_sum],
    )[0]


def enc_gradient(centered_a, centered_b, code_grad, after):
    half, width = centered_a.shape
    latents = code_grad.shape[1]

    def kernel(a_ref, b_ref, code_grad_ref, grad_ref):
        centered = jnp.concatenate([a_ref[...], b_ref[...]], axis=0)
        grad_ref[...] = lax.dot_general(
            centered, code_grad_ref[...], CONTRACT_FIRST, preferred_element_type=jnp.float32
        ).astype(jnp.bfloat16)

    return run(
        kernel,
        "enc_gradient",
        [((width, latents), jnp.bfloat16)],
        [centered_a, centered_b, code_grad],
        after,
        flops=4 * half * width * latents,
    )[0]


def dec_gradient(active_a, active_b, resid_a, resid_b, stored, after):
    half, latents = active_a.shape
    width = resid_a.shape[1]
    count = len(stored)

    def kernel(*refs):
        active_a_ref, active_b_ref, a_ref, b_ref = refs[:4]
        outs, grad_ref, sems = refs[5 + count : 5 + 2 * count], refs[-2], refs[-1]
        copies = [pltpu.make_async_copy(refs[4 + i], outs[i], sems.at[i]) for i in range(count)]
        for copy in copies:
            copy.start()
        active = jnp.concatenate([active_a_ref[...], active_b_ref[...]], axis=0)
        codes = (active * active).astype(jnp.bfloat16)
        resid = jnp.concatenate([a_ref[...], b_ref[...]], axis=0)
        grad_ref[...] = lax.dot_general(
            codes, resid, CONTRACT_FIRST, preferred_element_type=jnp.float32
        ).astype(jnp.bfloat16)
        for copy in copies:
            copy.wait()

    *outs, grad = pl.pallas_call(
        kernel,
        out_shape=[jax.ShapeDtypeStruct(a.shape, a.dtype) for a in stored] + [vmem((latents, width), jnp.bfloat16)],
        in_specs=[VMEM] * (5 + count),
        out_specs=[HBM] * count + [VMEM],
        scratch_shapes=[pltpu.SemaphoreType.DMA((count,))],
        compiler_params=pltpu.CompilerParams(vmem_limit_bytes=LIMIT),
        cost_estimate=pl.CostEstimate(flops=4 * half * latents * width, bytes_accessed=4 * latents * width, transcendentals=0),
        name="dec_gradient",
    )(*[in_vmem(a) for a in (active_a, active_b, resid_a, resid_b, *stored, after)])
    return outs, grad


def store(arrays, after):
    count = len(arrays)

    def kernel(*refs):
        outs, token_ref, sems = refs[count + 1 : 2 * count + 1], refs[-2], refs[-1]
        copies = [pltpu.make_async_copy(refs[i], outs[i], sems.at[i]) for i in range(count)]
        for copy in copies:
            copy.start()
        token_ref[...] = jnp.zeros_like(token_ref)
        for copy in copies:
            copy.wait()

    return pl.pallas_call(
        kernel,
        out_shape=[jax.ShapeDtypeStruct(a.shape, a.dtype) for a in arrays] + [vmem(*TOKEN)],
        in_specs=[VMEM] * (count + 1),
        out_specs=[HBM] * count + [VMEM],
        scratch_shapes=[pltpu.SemaphoreType.DMA((count,))],
        compiler_params=pltpu.CompilerParams(vmem_limit_bytes=LIMIT),
        cost_estimate=pl.CostEstimate(
            flops=0, bytes_accessed=2 * sum(a.size * a.dtype.itemsize for a in arrays), transcendentals=0
        ),
        name="store",
    )(*[in_vmem(a) for a in (*arrays, after)])


def add(*terms, after=(), order=None):
    order = order or list(range(len(terms)))

    def kernel(*refs):
        values = [refs[order.index(i)][...] for i in range(len(terms))]
        while len(values) > 1:
            values = [left + right for left, right in zip(values[::2], values[1::2])]
        refs[-1][...] = values[0]

    return run(kernel, "add", [(terms[0].shape, jnp.float32)], [terms[i] for i in order], after)[0]


def finish(terms, other, width, after):
    def kernel(terms_ref, other_ref, after_ref, bias_ref, loss_ref):
        total = terms_ref[...] + other_ref[...]
        bias_ref[...] = total[:, :width]
        loss_ref[...] = total[:, width : width + 1] / width

    return pl.pallas_call(
        kernel,
        out_shape=[jax.ShapeDtypeStruct((1, width), jnp.float32), jax.ShapeDtypeStruct((1, 1), jnp.float32)],
        in_specs=[VMEM] * 3,
        out_specs=[VMEM] * 2,
        compiler_params=pltpu.CompilerParams(vmem_limit_bytes=2 << 20),
        name="finish",
    )(in_vmem(terms), in_vmem(other), in_vmem(after))


def local(residuals, enc_weight, enc_bias, dec_weight, dec_bias):
    own_rows, width = residuals.shape
    lat = lax.axis_size("lat")
    row_count = own_rows * lat * lax.axis_size("sub")
    far, steps = plan(lat)

    enc_bias = enc_bias.reshape(1, -1)
    other = swap(residuals, far)
    siblings = swap(enc_weight, CORES), swap(enc_bias, CORES), swap(dec_weight, CORES)
    enc_vmem, own, dec_bias_row, enc_bias_row = load([enc_weight, residuals, dec_bias.reshape(1, width), enc_bias])
    paired = stack([own, other], after=[enc_vmem])
    (dec_vmem,) = load([dec_weight], after=[paired])
    rows = gather(paired, steps, ROWS_ORDER, after=[dec_vmem])
    centered_a, active_a, active_sibling, *parts = encode_decode(
        rows, [(enc_vmem, enc_bias_row, dec_vmem), siblings], dec_bias_row, len(steps[-1]) + 1
    )

    summed, dec_turned = halve(parts, steps[::-1], dec_vmem)
    active_b = swap(active_sibling, CORES)
    centered_b = swap(centered_a, CORES)
    enc_turned = turn(enc_vmem, [summed])
    error_args = summed, swap(summed, far), paired, dec_bias_row, row_count
    resid_bf = residual_gradient(*error_args, [enc_turned, active_b, centered_b])

    resid_a = gather(resid_bf, steps, RESID_ORDER)
    resid_b = swap(resid_a, CORES)
    recon, own_bias, square = own_terms(*error_args, [resid_bf])
    code_grad_bf, total = backward(resid_a, resid_b, dec_turned, active_a, active_b, row_count)
    terms = bias_product(total, enc_turned, own_bias, square, code_sum(active_a, active_b), row_count)

    grad_enc = enc_gradient(centered_a, centered_b, code_grad_bf, [terms])
    terms = add(terms, swap(terms, CORES), after=[grad_enc])
    (grad_enc, total), grad_dec = dec_gradient(active_a, active_b, resid_a, resid_b, [grad_enc, total], terms)
    for masks in steps:
        terms = add(
            terms,
            *[swap(terms, mask) for mask in masks],
            after=[grad_dec],
            order=[0, *TERMS_ORDER] if len(masks) > 1 else None,
        )
    grad_dec, recon, stored = store([grad_dec, recon], terms)
    grad_dec_bias, loss_value = finish(terms, swap(terms, far), width, stored)
    return recon, loss_value[0], grad_enc, total[0], grad_dec, grad_dec_bias[0]


def solution(mesh):
    placed = (
        P(("parts", "lat", "sub"), None),
        P(None, ("parts", "lat", "sub")),
        P(("parts", "lat", "sub")),
        P(("parts", "lat", "sub"), None),
        P("parts"),
    )
    return jax.shard_map(
        local,
        mesh=mesh,
        in_specs=placed,
        out_specs=(
            P(("parts", "lat", "sub"), None),
            P("parts"),
            P(None, ("parts", "lat", "sub")),
            P(("parts", "lat", "sub")),
            P(("parts", "lat", "sub"), None),
            P("parts"),
        ),
        check_vma=False,
    )
```

```python
import jax
import jax.numpy as jnp
from jax import lax
from jax.experimental import pallas as pl
from jax.experimental.pallas import tpu as pltpu
from jax.sharding import PartitionSpec as P

PENALTY = 0.2
CORES = 0
LANES = 128
LIMIT = 12 << 20
VMEM = pl.BlockSpec(memory_space=pltpu.VMEM)
HBM = pl.BlockSpec(memory_space=pltpu.HBM)
CONTRACT_FIRST = (((0,), (0,)), ((), ()))


def vmem(shape, dtype):
    return pltpu.VMEM(shape, dtype)


def in_vmem(array):
    return pltpu.with_memory_space_constraint(array, pltpu.VMEM)


def in_hbm(array):
    return pltpu.with_memory_space_constraint(array, pltpu.HBM)


TOKEN = ((8, LANES), jnp.float32)


def run(kernel, name, outs, args, after=(), flops=0, moved=0, limit=LIMIT):
    count = len(args)

    def body(*refs):
        kernel(*refs[:count], *refs[count + len(after) :])

    return pl.pallas_call(
        body,
        out_shape=[vmem(*out) for out in outs],
        in_specs=[VMEM] * (count + len(after)),
        out_specs=[VMEM] * len(outs),
        compiler_params=pltpu.CompilerParams(vmem_limit_bytes=limit),
        cost_estimate=pl.CostEstimate(flops=flops, bytes_accessed=moved, transcendentals=0),
        name=name,
    )(*[in_vmem(a) for a in args], *[in_vmem(a) for a in after])


def swap(values, mask):
    if mask == CORES:
        return lax.ppermute(values, "sub", [(i, i ^ 1) for i in range(2)])
    return lax.ppermute(values, "lat", [(i, i ^ mask) for i in range(lax.axis_size("lat"))])


ROWS_ORDER, SUM_ORDER, RESID_ORDER, TERMS_ORDER = (2, 3, 1), (2, 1, 3), (2, 3, 1), (2, 3, 1)


def plan(lat):
    bits = [1 << b for b in range(lat.bit_length() - 1)]
    near = bits[:-1]
    steps = [[1, 2, 3]] + [[b] for b in near[2:]] if len(near) > 1 else [[b] for b in near]
    return bits[-1], steps


def load(arrays, after=()):
    count = len(arrays)

    def kernel(*refs):
        copies = [
            pltpu.make_async_copy(refs[i], refs[count + len(after) + i], refs[-1].at[i]) for i in range(count)
        ]
        for copy in copies:
            copy.start()
        for copy in copies:
            copy.wait()

    return pl.pallas_call(
        kernel,
        out_shape=[vmem(array.shape, array.dtype) for array in arrays],
        in_specs=[HBM] * count + [VMEM] * len(after),
        out_specs=[VMEM] * count,
        scratch_shapes=[pltpu.SemaphoreType.DMA((count,))],
        compiler_params=pltpu.CompilerParams(vmem_limit_bytes=LIMIT),
        cost_estimate=pl.CostEstimate(
            flops=0, bytes_accessed=2 * sum(a.size * a.dtype.itemsize for a in arrays), transcendentals=0
        ),
        name="load",
    )(*[in_hbm(a) for a in arrays], *[in_vmem(a) for a in after])


def stack(blocks, after=(), order=None):
    width = blocks[0].shape[1]
    order = order or list(range(len(blocks)))

    def kernel(*refs):
        refs[-1][...] = jnp.concatenate([refs[order.index(i)][...] for i in range(len(blocks))], axis=0)

    shape = (sum(block.shape[0] for block in blocks), width)
    return run(kernel, "stack", [(shape, blocks[0].dtype)], [blocks[i] for i in order], after)[0]


def gather(rows, steps, order, after=()):
    for masks in steps:
        rows = stack([rows] + [swap(rows, mask) for mask in masks], after, [0, *order] if len(masks) > 1 else None)
    return rows


def add_parts(first, others, count, after=()):
    rows, width = first.shape
    size = rows // count

    def kernel(*refs):
        total = refs[0][...]
        for ref in refs[1 : 1 + len(others)]:
            total = total + ref[...]
        for part, ref in enumerate(refs[1 + len(others) :]):
            ref[...] = total[part * size : (part + 1) * size]

    return run(kernel, "add_parts", [((size, width), jnp.float32)] * count, [first, *others], after)


def halve(parts, steps, dec_weights):
    dec_turned = turn(dec_weights, 1, [parts[0]])
    for step, masks in enumerate(steps):
        others = [swap(part, mask) for part, mask in zip(parts[1:], masks)]
        if len(masks) > 1:
            others = [others[mask - 1] for mask in SUM_ORDER]
        count = len(steps[step + 1]) + 1 if step + 1 < len(steps) else 1
        parts = add_parts(parts[0], others, count, after=[dec_turned])
    return parts[0], dec_turned


def encode_decode(rows, weights, dec_bias, count):
    height, width = rows.shape
    latents = weights[0][0].shape[1]
    sets = len(weights)

    def kernel(rows_ref, dec_bias_ref, *refs):
        centered_ref, outs = refs[3 * sets], refs[3 * sets + 1 :]
        centered = (rows_ref[...].astype(jnp.float32) - dec_bias_ref[...]).astype(jnp.bfloat16)
        centered_ref[...] = centered
        codes = []
        for i in range(sets):
            enc_ref, enc_bias_ref = refs[3 * i], refs[3 * i + 1]
            preact = jnp.dot(centered, enc_ref[...], preferred_element_type=jnp.float32) + enc_bias_ref[...]
            active = jnp.maximum(preact, 0.0)
            outs[i][...] = active
            codes.append((active * active).astype(jnp.bfloat16))
        total = None
        for i in range(sets):
            partial = jnp.dot(codes[i], refs[3 * i + 2][...], preferred_element_type=jnp.float32)
            total = partial if total is None else total + partial
        size = height // count
        for part, ref in enumerate(outs[sets:]):
            ref[...] = total[part * size : (part + 1) * size]

    return run(
        kernel,
        "encode_decode",
        [((height, width), jnp.bfloat16)]
        + [((height, latents), jnp.float32)] * sets
        + [((height // count, width), jnp.float32)] * count,
        [rows, dec_bias, *[array for weight in weights for array in weight]],
        flops=4 * sets * height * width * latents,
    )


def code_sum(active_a, active_b):
    def kernel(a_ref, b_ref, sum_ref):
        total = jnp.sum(a_ref[...] * a_ref[...] + b_ref[...] * b_ref[...], keepdims=True)
        sum_ref[...] = jnp.broadcast_to(total, (1, LANES))

    return run(kernel, "code_sum", [((1, LANES), jnp.float32)], [active_a, active_b])[0]


def errors(summed_ref, other_ref, paired_ref, bias_ref):
    own = summed_ref.shape[0] // 2
    total = summed_ref[...] + jnp.concatenate([other_ref[own:], other_ref[:own]], axis=0)
    recon = total + bias_ref[...]
    return recon, recon - paired_ref[...].astype(jnp.float32)


def residual_gradient(summed, other, paired, dec_bias, row_count, after):
    def kernel(summed_ref, other_ref, paired_ref, bias_ref, resid_ref):
        _, error = errors(summed_ref, other_ref, paired_ref, bias_ref)
        resid_ref[...] = (2.0 / row_count * error).astype(jnp.bfloat16)

    return run(
        kernel, "residual_gradient", [(summed.shape, jnp.bfloat16)], [summed, other, paired, dec_bias], after
    )[0]


def own_terms(summed, other, paired, dec_bias, row_count, after):
    rows, width = summed.shape
    own = rows // 2

    def kernel(summed_ref, other_ref, paired_ref, bias_ref, recon_ref, own_ref, square_ref):
        recon, error = errors(summed_ref, other_ref, paired_ref, bias_ref)
        error = error[:own]
        recon_ref[...] = recon[:own].astype(jnp.bfloat16)
        own_ref[...] = jnp.sum(2.0 / row_count * error, axis=0, keepdims=True)
        square_ref[...] = jnp.broadcast_to(jnp.sum(error * error, keepdims=True), (1, LANES))

    return run(
        kernel,
        "own_terms",
        [((own, width), jnp.bfloat16), ((1, width), jnp.float32), ((1, LANES), jnp.float32)],
        [summed, other, paired, dec_bias],
        after,
    )


def turn(weights, axis, after):
    rows, columns = weights[0].shape
    count = len(weights)

    def kernel(*refs):
        turned_ref = refs[-1]
        for i in range(count):
            if axis == 0:
                turned_ref[i * columns : (i + 1) * columns] = refs[i][...].T
            else:
                turned_ref[:, i * rows : (i + 1) * rows] = refs[i][...].T

    shape = (count * columns, rows) if axis == 0 else (columns, count * rows)
    return run(
        kernel, "turn", [(shape, weights[0].dtype)], weights, after, moved=4 * count * rows * columns
    )[0]


def backward(resid, dec_turned, active_own, active_sibling, row_count):
    height = resid.shape[0]
    latents = active_own.shape[1]

    def kernel(resid_ref, dec_ref, own_ref, sibling_ref, own_grad_ref, sibling_grad_ref, total_ref):
        back = jnp.dot(resid_ref[...], dec_ref[...], preferred_element_type=jnp.float32)
        active = jnp.concatenate([own_ref[...], sibling_ref[...]], axis=1)
        code_grad = 2.0 * active * (back + PENALTY / row_count)
        own_grad_ref[...] = code_grad[:, :latents].astype(jnp.bfloat16)
        sibling_grad_ref[...] = code_grad[:, latents:]
        total_ref[...] = jnp.sum(code_grad, axis=0, keepdims=True)

    return run(
        kernel,
        "backward",
        [((height, latents), jnp.bfloat16), ((height, latents), jnp.float32), ((1, 2 * latents), jnp.float32)],
        [resid, dec_turned, active_own, active_sibling],
    )


def bias_product(total, enc_weight, own_bias, square, code_sum, row_count):
    latents, width = enc_weight.shape

    def kernel(total_ref, enc_ref, own_ref, square_ref, sum_ref, terms_ref):
        values = total_ref[...]
        high = values.astype(jnp.bfloat16).astype(jnp.float32)
        rest = values - high
        middle = rest.astype(jnp.bfloat16).astype(jnp.float32)
        pieces = [high, middle, rest - middle, jnp.zeros((5, latents), jnp.float32)]
        pieces = jnp.concatenate(pieces, axis=0).astype(jnp.bfloat16)
        product = jnp.dot(pieces, enc_ref[...], preferred_element_type=jnp.float32)
        terms_ref[:, :width] = own_ref[...] - (product[0:1] + (product[1:2] + product[2:3]))
        terms_ref[:, width:] = (square_ref[...] + PENALTY * sum_ref[...]) / row_count

    return run(
        kernel,
        "bias_product",
        [((1, width + LANES), jnp.float32)],
        [total, enc_weight, own_bias, square, code_sum],
    )[0]


def dec_gradient(active_a, active_b, resid_a, resid_b, after):
    half, latents = active_a.shape
    width = resid_a.shape[1]

    def kernel(active_a_ref, active_b_ref, a_ref, b_ref, grad_ref):
        active = jnp.concatenate([active_a_ref[...], active_b_ref[...]], axis=0)
        codes = (active * active).astype(jnp.bfloat16)
        resid = jnp.concatenate([a_ref[...], b_ref[...]], axis=0)
        grad_ref[...] = lax.dot_general(
            codes, resid, CONTRACT_FIRST, preferred_element_type=jnp.float32
        ).astype(jnp.bfloat16)

    return run(
        kernel,
        "dec_gradient",
        [((latents, width), jnp.bfloat16)],
        [active_a, active_b, resid_a, resid_b],
        after,
        flops=4 * half * width * latents,
    )[0]


def enc_gradient(centered_a, centered_b, code_grad_a, code_grad_b, total, stored, after):
    half, width = centered_a.shape
    latents = code_grad_a.shape[1]
    count = len(stored)

    def kernel(*refs):
        a_ref, b_ref, code_grad_a_ref, code_grad_b_ref, total_ref = refs[:5]
        outs, (grad_ref, bias_ref, sems) = refs[6 + count : 6 + 2 * count], refs[-3:]
        copies = [pltpu.make_async_copy(refs[5 + i], outs[i], sems.at[i]) for i in range(count)]
        for copy in copies:
            copy.start()
        grad_b = code_grad_b_ref[...]
        bias_ref[...] = total_ref[:, :latents] + jnp.sum(grad_b, axis=0, keepdims=True)
        centered = jnp.concatenate([a_ref[...], b_ref[...]], axis=0)
        code_grad = jnp.concatenate([code_grad_a_ref[...], grad_b.astype(jnp.bfloat16)], axis=0)
        grad_ref[...] = lax.dot_general(
            centered, code_grad, CONTRACT_FIRST, preferred_element_type=jnp.float32
        ).astype(jnp.bfloat16)
        for copy in copies:
            copy.wait()

    *outs, grad, bias = pl.pallas_call(
        kernel,
        out_shape=[jax.ShapeDtypeStruct(a.shape, a.dtype) for a in stored]
        + [vmem((width, latents), jnp.bfloat16), vmem((1, latents), jnp.float32)],
        in_specs=[VMEM] * (6 + count),
        out_specs=[HBM] * count + [VMEM] * 2,
        scratch_shapes=[pltpu.SemaphoreType.DMA((count,))],
        compiler_params=pltpu.CompilerParams(vmem_limit_bytes=LIMIT),
        cost_estimate=pl.CostEstimate(flops=4 * half * latents * width, bytes_accessed=4 * latents * width, transcendentals=0),
        name="enc_gradient",
    )(*[in_vmem(a) for a in (centered_a, centered_b, code_grad_a, code_grad_b, total, *stored, after)])
    return outs, grad, bias


def store(arrays, after):
    count = len(arrays)

    def kernel(*refs):
        outs, token_ref, sems = refs[count + 1 : 2 * count + 1], refs[-2], refs[-1]
        copies = [pltpu.make_async_copy(refs[i], outs[i], sems.at[i]) for i in range(count)]
        for copy in copies:
            copy.start()
        token_ref[...] = jnp.zeros_like(token_ref)
        for copy in copies:
            copy.wait()

    return pl.pallas_call(
        kernel,
        out_shape=[jax.ShapeDtypeStruct(a.shape, a.dtype) for a in arrays] + [vmem(*TOKEN)],
        in_specs=[VMEM] * (count + 1),
        out_specs=[HBM] * count + [VMEM],
        scratch_shapes=[pltpu.SemaphoreType.DMA((count,))],
        compiler_params=pltpu.CompilerParams(vmem_limit_bytes=LIMIT),
        cost_estimate=pl.CostEstimate(
            flops=0, bytes_accessed=2 * sum(a.size * a.dtype.itemsize for a in arrays), transcendentals=0
        ),
        name="store",
    )(*[in_vmem(a) for a in (*arrays, after)])


def add(*terms, after=(), order=None):
    order = order or list(range(len(terms)))

    def kernel(*refs):
        values = [refs[order.index(i)][...] for i in range(len(terms))]
        while len(values) > 1:
            values = [left + right for left, right in zip(values[::2], values[1::2])]
        refs[-1][...] = values[0]

    return run(kernel, "add", [(terms[0].shape, jnp.float32)], [terms[i] for i in order], after)[0]


def finish(terms, other, width, after):
    def kernel(terms_ref, other_ref, after_ref, bias_ref, loss_ref):
        total = terms_ref[...] + other_ref[...]
        bias_ref[...] = total[:, :width]
        loss_ref[...] = total[:, width : width + 1] / width

    return pl.pallas_call(
        kernel,
        out_shape=[jax.ShapeDtypeStruct((1, width), jnp.float32), jax.ShapeDtypeStruct((1, 1), jnp.float32)],
        in_specs=[VMEM] * 3,
        out_specs=[VMEM] * 2,
        compiler_params=pltpu.CompilerParams(vmem_limit_bytes=2 << 20),
        name="finish",
    )(in_vmem(terms), in_vmem(other), in_vmem(after))


def local(residuals, enc_weight, enc_bias, dec_weight, dec_bias):
    own_rows, width = residuals.shape
    lat = lax.axis_size("lat")
    row_count = own_rows * lat * lax.axis_size("sub")
    far, steps = plan(lat)

    enc_bias = enc_bias.reshape(1, -1)
    other = swap(residuals, far)
    siblings = swap(enc_weight, CORES), swap(enc_bias, CORES), swap(dec_weight, CORES)
    enc_vmem, own, dec_bias_row, enc_bias_row = load([enc_weight, residuals, dec_bias.reshape(1, width), enc_bias])
    paired = stack([own, other], after=[enc_vmem])
    (dec_vmem,) = load([dec_weight], after=[paired])
    rows = gather(paired, steps, ROWS_ORDER, after=[dec_vmem])
    centered_a, active_a, active_sibling, *parts = encode_decode(
        rows, [(enc_vmem, enc_bias_row, dec_vmem), siblings], dec_bias_row, len(steps[-1]) + 1
    )

    summed, dec_turned = halve(parts, steps[::-1], [dec_vmem, siblings[2]])
    active_b = swap(active_sibling, CORES)
    centered_b = swap(centered_a, CORES)
    enc_turned = turn([enc_vmem, siblings[0]], 0, [summed])
    error_args = summed, swap(summed, far), paired, dec_bias_row, row_count
    resid_bf = residual_gradient(*error_args, [enc_turned, active_b, centered_b])

    recon, own_bias, square = own_terms(*error_args, [resid_bf])
    code_total = code_sum(active_a, active_b)
    resid_a = gather(resid_bf, steps, RESID_ORDER, after=[square, code_total])
    resid_b = swap(resid_a, CORES)
    code_grad_a, code_grad_sibling, total = backward(resid_a, dec_turned, active_a, active_sibling, row_count)
    terms = bias_product(total, enc_turned, own_bias, square, code_total, row_count)
    code_grad_b = swap(code_grad_sibling, CORES)

    grad_dec = dec_gradient(active_a, active_b, resid_a, resid_b, [terms])
    terms = add(terms, swap(terms, CORES), after=[grad_dec])
    (grad_dec, recon), grad_enc, grad_enc_bias = enc_gradient(
        centered_a, centered_b, code_grad_a, code_grad_b, total, [grad_dec, recon], terms
    )
    for masks in steps:
        terms = add(
            terms,
            *[swap(terms, mask) for mask in masks],
            after=[grad_enc],
            order=[0, *TERMS_ORDER] if len(masks) > 1 else None,
        )
    grad_enc, grad_enc_bias, stored = store([grad_enc, grad_enc_bias], terms)
    grad_dec_bias, loss_value = finish(terms, swap(terms, far), width, stored)
    return recon, loss_value[0], grad_enc, grad_enc_bias[0], grad_dec, grad_dec_bias[0]


def solution(mesh):
    placed = (
        P(("parts", "lat", "sub"), None),
        P(None, ("parts", "lat", "sub")),
        P(("parts", "lat", "sub")),
        P(("parts", "lat", "sub"), None),
        P("parts"),
    )
    return jax.shard_map(
        local,
        mesh=mesh,
        in_specs=placed,
        out_specs=(
            P(("parts", "lat", "sub"), None),
            P("parts"),
            P(None, ("parts", "lat", "sub")),
            P(("parts", "lat", "sub")),
            P(("parts", "lat", "sub"), None),
            P("parts"),
        ),
        check_vma=False,
    )
```

```python
import jax
import jax.numpy as jnp
from jax import lax
from jax.experimental import pallas as pl
from jax.experimental.pallas import tpu as pltpu
from jax.sharding import PartitionSpec as P

PENALTY = 0.2
CORES = 0
LANES = 128
LIMIT = 12 << 20
VMEM = pl.BlockSpec(memory_space=pltpu.VMEM)
HBM = pl.BlockSpec(memory_space=pltpu.HBM)
CONTRACT_FIRST = (((0,), (0,)), ((), ()))


def vmem(shape, dtype):
    return pltpu.VMEM(shape, dtype)


def in_vmem(array):
    return pltpu.with_memory_space_constraint(array, pltpu.VMEM)


def in_hbm(array):
    return pltpu.with_memory_space_constraint(array, pltpu.HBM)


TOKEN = ((8, LANES), jnp.float32)


def run(kernel, name, outs, args, after=(), flops=0, moved=0, limit=LIMIT):
    count = len(args)

    def body(*refs):
        kernel(*refs[:count], *refs[count + len(after) :])

    return pl.pallas_call(
        body,
        out_shape=[vmem(*out) for out in outs],
        in_specs=[VMEM] * (count + len(after)),
        out_specs=[VMEM] * len(outs),
        compiler_params=pltpu.CompilerParams(vmem_limit_bytes=limit),
        cost_estimate=pl.CostEstimate(flops=flops, bytes_accessed=moved, transcendentals=0),
        name=name,
    )(*[in_vmem(a) for a in args], *[in_vmem(a) for a in after])


def swap(values, mask):
    if mask == CORES:
        return lax.ppermute(values, "sub", [(i, i ^ 1) for i in range(2)])
    return lax.ppermute(values, "lat", [(i, i ^ mask) for i in range(lax.axis_size("lat"))])


ROWS_ORDER, SUM_ORDER, RESID_ORDER, TERMS_ORDER = (2, 3, 1), (2, 1, 3), (2, 3, 1), (2, 3, 1)


def plan(lat):
    bits = [1 << b for b in range(lat.bit_length() - 1)]
    near = bits[:-1]
    steps = [[1, 2, 3]] + [[b] for b in near[2:]] if len(near) > 1 else [[b] for b in near]
    return bits[-1], steps


def load(arrays, after=()):
    count = len(arrays)

    def kernel(*refs):
        copies = [
            pltpu.make_async_copy(refs[i], refs[count + len(after) + i], refs[-1].at[i]) for i in range(count)
        ]
        for copy in copies:
            copy.start()
        for copy in copies:
            copy.wait()

    return pl.pallas_call(
        kernel,
        out_shape=[vmem(array.shape, array.dtype) for array in arrays],
        in_specs=[HBM] * count + [VMEM] * len(after),
        out_specs=[VMEM] * count,
        scratch_shapes=[pltpu.SemaphoreType.DMA((count,))],
        compiler_params=pltpu.CompilerParams(vmem_limit_bytes=LIMIT),
        cost_estimate=pl.CostEstimate(
            flops=0, bytes_accessed=2 * sum(a.size * a.dtype.itemsize for a in arrays), transcendentals=0
        ),
        name="load",
    )(*[in_hbm(a) for a in arrays], *[in_vmem(a) for a in after])


def stack(blocks, after=(), order=None):
    width = blocks[0].shape[1]
    order = order or list(range(len(blocks)))

    def kernel(*refs):
        refs[-1][...] = jnp.concatenate([refs[order.index(i)][...] for i in range(len(blocks))], axis=0)

    shape = (sum(block.shape[0] for block in blocks), width)
    return run(kernel, "stack", [(shape, blocks[0].dtype)], [blocks[i] for i in order], after)[0]


def gather(rows, steps, order, after=()):
    for masks in steps:
        rows = stack([rows] + [swap(rows, mask) for mask in masks], after, [0, *order] if len(masks) > 1 else None)
    return rows


def add_parts(first, others, count, after=()):
    rows, width = first.shape
    size = rows // count

    def kernel(*refs):
        total = refs[0][...]
        for ref in refs[1 : 1 + len(others)]:
            total = total + ref[...]
        for part, ref in enumerate(refs[1 + len(others) :]):
            ref[...] = total[part * size : (part + 1) * size]

    return run(kernel, "add_parts", [((size, width), jnp.float32)] * count, [first, *others], after)


def halve(parts, steps, dec_weights):
    dec_turned = turn(dec_weights, 1, [parts[0]])
    for step, masks in enumerate(steps):
        others = [swap(part, mask) for part, mask in zip(parts[1:], masks)]
        if len(masks) > 1:
            others = [others[mask - 1] for mask in SUM_ORDER]
        count = len(steps[step + 1]) + 1 if step + 1 < len(steps) else 1
        parts = add_parts(parts[0], others, count, after=[dec_turned])
    return parts[0], dec_turned


def encode_decode(rows, weights, dec_bias, count):
    height, width = rows.shape
    latents = weights[0][0].shape[1]
    sets = len(weights)

    def kernel(rows_ref, dec_bias_ref, *refs):
        centered_ref, outs = refs[3 * sets], refs[3 * sets + 1 :]
        centered = (rows_ref[...].astype(jnp.float32) - dec_bias_ref[...]).astype(jnp.bfloat16)
        centered_ref[...] = centered
        codes = []
        for i in range(sets):
            enc_ref, enc_bias_ref = refs[3 * i], refs[3 * i + 1]
            preact = jnp.dot(centered, enc_ref[...], preferred_element_type=jnp.float32) + enc_bias_ref[...]
            active = jnp.maximum(preact, 0.0)
            outs[i][...] = active
            codes.append((active * active).astype(jnp.bfloat16))
        total = None
        for i in range(sets):
            partial = jnp.dot(codes[i], refs[3 * i + 2][...], preferred_element_type=jnp.float32)
            total = partial if total is None else total + partial
        size = height // count
        for part, ref in enumerate(outs[sets:]):
            ref[...] = total[part * size : (part + 1) * size]

    return run(
        kernel,
        "encode_decode",
        [((height, width), jnp.bfloat16)]
        + [((height, latents), jnp.float32)] * sets
        + [((height // count, width), jnp.float32)] * count,
        [rows, dec_bias, *[array for weight in weights for array in weight]],
        flops=4 * sets * height * width * latents,
    )


def code_sum(active_a, active_b):
    def kernel(a_ref, b_ref, sum_ref):
        total = jnp.sum(a_ref[...] * a_ref[...] + b_ref[...] * b_ref[...], keepdims=True)
        sum_ref[...] = jnp.broadcast_to(total, (1, LANES))

    return run(kernel, "code_sum", [((1, LANES), jnp.float32)], [active_a, active_b])[0]


def errors(summed_ref, other_ref, paired_ref, bias_ref):
    own = summed_ref.shape[0] // 2
    total = summed_ref[...] + jnp.concatenate([other_ref[own:], other_ref[:own]], axis=0)
    recon = total + bias_ref[...]
    return recon, recon - paired_ref[...].astype(jnp.float32)


def residual_gradient(summed, other, paired, dec_bias, row_count, after):
    def kernel(summed_ref, other_ref, paired_ref, bias_ref, resid_ref):
        _, error = errors(summed_ref, other_ref, paired_ref, bias_ref)
        resid_ref[...] = (2.0 / row_count * error).astype(jnp.bfloat16)

    return run(
        kernel, "residual_gradient", [(summed.shape, jnp.bfloat16)], [summed, other, paired, dec_bias], after
    )[0]


def own_terms(summed, other, paired, dec_bias, row_count, after):
    rows, width = summed.shape
    own = rows // 2

    def kernel(summed_ref, other_ref, paired_ref, bias_ref, recon_ref, own_ref, square_ref):
        recon, error = errors(summed_ref, other_ref, paired_ref, bias_ref)
        error = error[:own]
        recon_ref[...] = recon[:own].astype(jnp.bfloat16)
        own_ref[...] = jnp.sum(2.0 / row_count * error, axis=0, keepdims=True)
        square_ref[...] = jnp.broadcast_to(jnp.sum(error * error, keepdims=True), (1, LANES))

    return run(
        kernel,
        "own_terms",
        [((own, width), jnp.bfloat16), ((1, width), jnp.float32), ((1, LANES), jnp.float32)],
        [summed, other, paired, dec_bias],
        after,
    )


def turn(weights, axis, after):
    rows, columns = weights[0].shape
    count = len(weights)

    def kernel(*refs):
        turned_ref = refs[-1]
        for i in range(count):
            if axis == 0:
                turned_ref[i * columns : (i + 1) * columns] = refs[i][...].T
            else:
                turned_ref[:, i * rows : (i + 1) * rows] = refs[i][...].T

    shape = (count * columns, rows) if axis == 0 else (columns, count * rows)
    return run(
        kernel, "turn", [(shape, weights[0].dtype)], weights, after, moved=4 * count * rows * columns
    )[0]


def backward(resid, dec_turned, active_own, active_sibling, row_count):
    height = resid.shape[0]
    latents = active_own.shape[1]

    def kernel(resid_ref, dec_ref, own_ref, sibling_ref, own_grad_ref, total_ref):
        back = jnp.dot(resid_ref[...], dec_ref[...], preferred_element_type=jnp.float32)
        active = jnp.concatenate([own_ref[...], sibling_ref[...]], axis=1)
        code_grad = 2.0 * active * (back + PENALTY / row_count)
        own_grad_ref[...] = code_grad[:, :latents].astype(jnp.bfloat16)
        total_ref[...] = jnp.sum(code_grad, axis=0, keepdims=True)

    return run(
        kernel,
        "backward",
        [((height, latents), jnp.bfloat16), ((1, 2 * latents), jnp.float32)],
        [resid, dec_turned, active_own, active_sibling],
    )


def bias_product(total, enc_weight, own_bias, square, code_sum, row_count):
    latents, width = enc_weight.shape

    def kernel(total_ref, enc_ref, own_ref, square_ref, sum_ref, terms_ref):
        values = total_ref[...]
        high = values.astype(jnp.bfloat16).astype(jnp.float32)
        rest = values - high
        middle = rest.astype(jnp.bfloat16).astype(jnp.float32)
        pieces = [high, middle, rest - middle, jnp.zeros((5, latents), jnp.float32)]
        pieces = jnp.concatenate(pieces, axis=0).astype(jnp.bfloat16)
        product = jnp.dot(pieces, enc_ref[...], preferred_element_type=jnp.float32)
        terms_ref[:, :width] = own_ref[...] - (product[0:1] + (product[1:2] + product[2:3]))
        terms_ref[:, width:] = (square_ref[...] + PENALTY * sum_ref[...]) / row_count

    return run(
        kernel,
        "bias_product",
        [((1, width + LANES), jnp.float32)],
        [total, enc_weight, own_bias, square, code_sum],
    )[0]


def dec_gradient(active_a, active_b, resid_a, resid_b, after):
    half, latents = active_a.shape
    width = resid_a.shape[1]

    def kernel(active_a_ref, active_b_ref, a_ref, b_ref, grad_ref):
        active = jnp.concatenate([active_a_ref[...], active_b_ref[...]], axis=0)
        codes = (active * active).astype(jnp.bfloat16)
        resid = jnp.concatenate([a_ref[...], b_ref[...]], axis=0)
        grad_ref[...] = lax.dot_general(
            codes, resid, CONTRACT_FIRST, preferred_element_type=jnp.float32
        ).astype(jnp.bfloat16)

    return run(
        kernel,
        "dec_gradient",
        [((latents, width), jnp.bfloat16)],
        [active_a, active_b, resid_a, resid_b],
        after,
        flops=4 * half * width * latents,
    )[0]


def enc_gradient(centered_a, centered_b, code_grad_a, resid_b, dec_turned, active_b, total, row_count, stored, after):
    half, width = centered_a.shape
    latents = code_grad_a.shape[1]
    count = len(stored)

    def kernel(*refs):
        a_ref, b_ref, code_grad_a_ref, resid_ref, dec_ref, active_ref, total_ref = refs[:7]
        outs, (grad_ref, bias_ref, sems) = refs[8 + count : 8 + 2 * count], refs[-3:]
        copies = [pltpu.make_async_copy(refs[7 + i], outs[i], sems.at[i]) for i in range(count)]
        for copy in copies:
            copy.start()
        back = jnp.dot(resid_ref[...], dec_ref[:, :latents], preferred_element_type=jnp.float32)
        grad_b = 2.0 * active_ref[...] * (back + PENALTY / row_count)
        bias_ref[...] = total_ref[:, :latents] + jnp.sum(grad_b, axis=0, keepdims=True)
        centered = jnp.concatenate([a_ref[...], b_ref[...]], axis=0)
        code_grad = jnp.concatenate([code_grad_a_ref[...], grad_b.astype(jnp.bfloat16)], axis=0)
        grad_ref[...] = lax.dot_general(
            centered, code_grad, CONTRACT_FIRST, preferred_element_type=jnp.float32
        ).astype(jnp.bfloat16)
        for copy in copies:
            copy.wait()

    *outs, grad, bias = pl.pallas_call(
        kernel,
        out_shape=[jax.ShapeDtypeStruct(a.shape, a.dtype) for a in stored]
        + [vmem((width, latents), jnp.bfloat16), vmem((1, latents), jnp.float32)],
        in_specs=[VMEM] * (8 + count),
        out_specs=[HBM] * count + [VMEM] * 2,
        scratch_shapes=[pltpu.SemaphoreType.DMA((count,))],
        compiler_params=pltpu.CompilerParams(vmem_limit_bytes=LIMIT),
        cost_estimate=pl.CostEstimate(flops=4 * half * latents * width, bytes_accessed=4 * latents * width, transcendentals=0),
        name="enc_gradient",
    )(*[in_vmem(a) for a in (centered_a, centered_b, code_grad_a, resid_b, dec_turned, active_b, total, *stored, after)])
    return outs, grad, bias


def store(arrays, after):
    count = len(arrays)

    def kernel(*refs):
        outs, token_ref, sems = refs[count + 1 : 2 * count + 1], refs[-2], refs[-1]
        copies = [pltpu.make_async_copy(refs[i], outs[i], sems.at[i]) for i in range(count)]
        for copy in copies:
            copy.start()
        token_ref[...] = jnp.zeros_like(token_ref)
        for copy in copies:
            copy.wait()

    return pl.pallas_call(
        kernel,
        out_shape=[jax.ShapeDtypeStruct(a.shape, a.dtype) for a in arrays] + [vmem(*TOKEN)],
        in_specs=[VMEM] * (count + 1),
        out_specs=[HBM] * count + [VMEM],
        scratch_shapes=[pltpu.SemaphoreType.DMA((count,))],
        compiler_params=pltpu.CompilerParams(vmem_limit_bytes=LIMIT),
        cost_estimate=pl.CostEstimate(
            flops=0, bytes_accessed=2 * sum(a.size * a.dtype.itemsize for a in arrays), transcendentals=0
        ),
        name="store",
    )(*[in_vmem(a) for a in (*arrays, after)])


def add(*terms, after=(), order=None):
    order = order or list(range(len(terms)))

    def kernel(*refs):
        values = [refs[order.index(i)][...] for i in range(len(terms))]
        while len(values) > 1:
            values = [left + right for left, right in zip(values[::2], values[1::2])]
        refs[-1][...] = values[0]

    return run(kernel, "add", [(terms[0].shape, jnp.float32)], [terms[i] for i in order], after)[0]


def finish(terms, other, width, after):
    def kernel(terms_ref, other_ref, after_ref, bias_ref, loss_ref):
        total = terms_ref[...] + other_ref[...]
        bias_ref[...] = total[:, :width]
        loss_ref[...] = total[:, width : width + 1] / width

    return pl.pallas_call(
        kernel,
        out_shape=[jax.ShapeDtypeStruct((1, width), jnp.float32), jax.ShapeDtypeStruct((1, 1), jnp.float32)],
        in_specs=[VMEM] * 3,
        out_specs=[VMEM] * 2,
        compiler_params=pltpu.CompilerParams(vmem_limit_bytes=2 << 20),
        name="finish",
    )(in_vmem(terms), in_vmem(other), in_vmem(after))


def local(residuals, enc_weight, enc_bias, dec_weight, dec_bias):
    own_rows, width = residuals.shape
    lat = lax.axis_size("lat")
    row_count = own_rows * lat * lax.axis_size("sub")
    far, steps = plan(lat)

    enc_bias = enc_bias.reshape(1, -1)
    other = swap(residuals, far)
    siblings = swap(enc_weight, CORES), swap(enc_bias, CORES), swap(dec_weight, CORES)
    enc_vmem, own, dec_bias_row, enc_bias_row = load([enc_weight, residuals, dec_bias.reshape(1, width), enc_bias])
    paired = stack([own, other], after=[enc_vmem])
    (dec_vmem,) = load([dec_weight], after=[paired])
    rows = gather(paired, steps, ROWS_ORDER, after=[dec_vmem])
    centered_a, active_a, active_sibling, *parts = encode_decode(
        rows, [(enc_vmem, enc_bias_row, dec_vmem), siblings], dec_bias_row, len(steps[-1]) + 1
    )

    summed, dec_turned = halve(parts, steps[::-1], [dec_vmem, siblings[2]])
    active_b = swap(active_sibling, CORES)
    centered_b = swap(centered_a, CORES)
    enc_turned = turn([enc_vmem, siblings[0]], 0, [summed])
    error_args = summed, swap(summed, far), paired, dec_bias_row, row_count
    resid_bf = residual_gradient(*error_args, [enc_turned, active_b, centered_b])

    recon, own_bias, square = own_terms(*error_args, [resid_bf])
    code_total = code_sum(active_a, active_b)
    resid_a = gather(resid_bf, steps, RESID_ORDER, after=[square, code_total])
    resid_b = swap(resid_a, CORES)
    code_grad_a, total = backward(resid_a, dec_turned, active_a, active_sibling, row_count)
    terms = bias_product(total, enc_turned, own_bias, square, code_total, row_count)

    grad_dec = dec_gradient(active_a, active_b, resid_a, resid_b, [terms])
    terms = add(terms, swap(terms, CORES), after=[grad_dec])
    (grad_dec, recon), grad_enc, grad_enc_bias = enc_gradient(
        centered_a, centered_b, code_grad_a, resid_b, dec_turned, active_b, total, row_count, [grad_dec, recon], terms
    )
    for masks in steps:
        terms = add(
            terms,
            *[swap(terms, mask) for mask in masks],
            after=[grad_enc],
            order=[0, *TERMS_ORDER] if len(masks) > 1 else None,
        )
    grad_enc, grad_enc_bias, stored = store([grad_enc, grad_enc_bias], terms)
    grad_dec_bias, loss_value = finish(terms, swap(terms, far), width, stored)
    return recon, loss_value[0], grad_enc, grad_enc_bias[0], grad_dec, grad_dec_bias[0]


def solution(mesh):
    placed = (
        P(("parts", "lat", "sub"), None),
        P(None, ("parts", "lat", "sub")),
        P(("parts", "lat", "sub")),
        P(("parts", "lat", "sub"), None),
        P("parts"),
    )
    return jax.shard_map(
        local,
        mesh=mesh,
        in_specs=placed,
        out_specs=(
            P(("parts", "lat", "sub"), None),
            P("parts"),
            P(None, ("parts", "lat", "sub")),
            P(("parts", "lat", "sub")),
            P(("parts", "lat", "sub"), None),
            P("parts"),
        ),
        check_vma=False,
    )
```

```python
import jax
import jax.numpy as jnp
from jax import lax
from jax.experimental import pallas as pl
from jax.experimental.pallas import tpu as pltpu
from jax.sharding import PartitionSpec as P

PENALTY = 0.2
CORES = 0
LANES = 128
LIMIT = 12 << 20
VMEM = pl.BlockSpec(memory_space=pltpu.VMEM)
HBM = pl.BlockSpec(memory_space=pltpu.HBM)
CONTRACT_FIRST = (((0,), (0,)), ((), ()))


def vmem(shape, dtype):
    return pltpu.VMEM(shape, dtype)


def in_vmem(array):
    return pltpu.with_memory_space_constraint(array, pltpu.VMEM)


def in_hbm(array):
    return pltpu.with_memory_space_constraint(array, pltpu.HBM)


TOKEN = ((8, LANES), jnp.float32)


def run(kernel, name, outs, args, after=(), flops=0, moved=0, limit=LIMIT):
    count = len(args)

    def body(*refs):
        kernel(*refs[:count], *refs[count + len(after) :])

    return pl.pallas_call(
        body,
        out_shape=[vmem(*out) for out in outs],
        in_specs=[VMEM] * (count + len(after)),
        out_specs=[VMEM] * len(outs),
        compiler_params=pltpu.CompilerParams(vmem_limit_bytes=limit),
        cost_estimate=pl.CostEstimate(flops=flops, bytes_accessed=moved, transcendentals=0),
        name=name,
    )(*[in_vmem(a) for a in args], *[in_vmem(a) for a in after])


def swap(values, mask):
    if mask == CORES:
        return lax.ppermute(values, "sub", [(i, i ^ 1) for i in range(2)])
    return lax.ppermute(values, "lat", [(i, i ^ mask) for i in range(lax.axis_size("lat"))])


ROWS_ORDER, SUM_ORDER, RESID_ORDER, TERMS_ORDER = (2, 3, 1), (2, 1, 3), (2, 3, 1), (2, 3, 1)


def plan(lat):
    bits = [1 << b for b in range(lat.bit_length() - 1)]
    near = bits[:-1]
    steps = [[1, 2, 3]] + [[b] for b in near[2:]] if len(near) > 1 else [[b] for b in near]
    return bits[-1], steps


def load(arrays, after=()):
    count = len(arrays)

    def kernel(*refs):
        copies = [
            pltpu.make_async_copy(refs[i], refs[count + len(after) + i], refs[-1].at[i]) for i in range(count)
        ]
        for copy in copies:
            copy.start()
        for copy in copies:
            copy.wait()

    return pl.pallas_call(
        kernel,
        out_shape=[vmem(array.shape, array.dtype) for array in arrays],
        in_specs=[HBM] * count + [VMEM] * len(after),
        out_specs=[VMEM] * count,
        scratch_shapes=[pltpu.SemaphoreType.DMA((count,))],
        compiler_params=pltpu.CompilerParams(vmem_limit_bytes=LIMIT),
        cost_estimate=pl.CostEstimate(
            flops=0, bytes_accessed=2 * sum(a.size * a.dtype.itemsize for a in arrays), transcendentals=0
        ),
        name="load",
    )(*[in_hbm(a) for a in arrays], *[in_vmem(a) for a in after])


def stack(blocks, after=(), order=None):
    width = blocks[0].shape[1]
    order = order or list(range(len(blocks)))

    def kernel(*refs):
        refs[-1][...] = jnp.concatenate([refs[order.index(i)][...] for i in range(len(blocks))], axis=0)

    shape = (sum(block.shape[0] for block in blocks), width)
    return run(kernel, "stack", [(shape, blocks[0].dtype)], [blocks[i] for i in order], after)[0]


def gather(rows, steps, order, after=()):
    for masks in steps:
        rows = stack([rows] + [swap(rows, mask) for mask in masks], after, [0, *order] if len(masks) > 1 else None)
    return rows


def add_parts(first, others, count, after=()):
    rows, width = first.shape
    size = rows // count

    def kernel(*refs):
        total = refs[0][...]
        for ref in refs[1 : 1 + len(others)]:
            total = total + ref[...]
        for part, ref in enumerate(refs[1 + len(others) :]):
            ref[...] = total[part * size : (part + 1) * size]

    return run(kernel, "add_parts", [((size, width), jnp.float32)] * count, [first, *others], after)


def halve(parts, steps, dec_weights):
    dec_turned = turn(dec_weights, 1, [parts[0]])
    for step, masks in enumerate(steps):
        others = [swap(part, mask) for part, mask in zip(parts[1:], masks)]
        if len(masks) > 1:
            others = [others[mask - 1] for mask in SUM_ORDER]
        count = len(steps[step + 1]) + 1 if step + 1 < len(steps) else 1
        parts = add_parts(parts[0], others, count, after=[dec_turned])
    return parts[0], dec_turned


def encode_decode(rows, weights, dec_bias, count):
    height, width = rows.shape
    latents = weights[0][0].shape[1]
    sets = len(weights)

    def kernel(rows_ref, dec_bias_ref, *refs):
        centered_ref, outs = refs[3 * sets], refs[3 * sets + 1 :]
        centered = (rows_ref[...].astype(jnp.float32) - dec_bias_ref[...]).astype(jnp.bfloat16)
        centered_ref[...] = centered
        codes = []
        for i in range(sets):
            enc_ref, enc_bias_ref = refs[3 * i], refs[3 * i + 1]
            preact = jnp.dot(centered, enc_ref[...], preferred_element_type=jnp.float32) + enc_bias_ref[...]
            active = jnp.maximum(preact, 0.0)
            outs[i][...] = active
            codes.append((active * active).astype(jnp.bfloat16))
        total = None
        for i in range(sets):
            partial = jnp.dot(codes[i], refs[3 * i + 2][...], preferred_element_type=jnp.float32)
            total = partial if total is None else total + partial
        size = height // count
        for part, ref in enumerate(outs[sets:]):
            ref[...] = total[part * size : (part + 1) * size]

    return run(
        kernel,
        "encode_decode",
        [((height, width), jnp.bfloat16)]
        + [((height, latents), jnp.float32)] * sets
        + [((height // count, width), jnp.float32)] * count,
        [rows, dec_bias, *[array for weight in weights for array in weight]],
        flops=4 * sets * height * width * latents,
    )


def code_sum(active_a, active_b):
    def kernel(a_ref, b_ref, sum_ref):
        total = jnp.sum(a_ref[...] * a_ref[...] + b_ref[...] * b_ref[...], keepdims=True)
        sum_ref[...] = jnp.broadcast_to(total, (1, LANES))

    return run(kernel, "code_sum", [((1, LANES), jnp.float32)], [active_a, active_b])[0]


def errors(summed_ref, other_ref, paired_ref, bias_ref):
    own = summed_ref.shape[0] // 2
    total = summed_ref[...] + jnp.concatenate([other_ref[own:], other_ref[:own]], axis=0)
    recon = total + bias_ref[...]
    return recon, recon - paired_ref[...].astype(jnp.float32)


def residual_gradient(summed, other, paired, dec_bias, row_count, after):
    def kernel(summed_ref, other_ref, paired_ref, bias_ref, resid_ref):
        _, error = errors(summed_ref, other_ref, paired_ref, bias_ref)
        resid_ref[...] = (2.0 / row_count * error).astype(jnp.bfloat16)

    return run(
        kernel, "residual_gradient", [(summed.shape, jnp.bfloat16)], [summed, other, paired, dec_bias], after
    )[0]


def own_terms(summed, other, paired, dec_bias, row_count, after):
    rows, width = summed.shape
    own = rows // 2

    def kernel(summed_ref, other_ref, paired_ref, bias_ref, recon_ref, own_ref, square_ref):
        recon, error = errors(summed_ref, other_ref, paired_ref, bias_ref)
        error = error[:own]
        recon_ref[...] = recon[:own].astype(jnp.bfloat16)
        own_ref[...] = jnp.sum(2.0 / row_count * error, axis=0, keepdims=True)
        square_ref[...] = jnp.broadcast_to(jnp.sum(error * error, keepdims=True), (1, LANES))

    return run(
        kernel,
        "own_terms",
        [((own, width), jnp.bfloat16), ((1, width), jnp.float32), ((1, LANES), jnp.float32)],
        [summed, other, paired, dec_bias],
        after,
    )


def turn(weights, axis, after):
    rows, columns = weights[0].shape
    count = len(weights)

    def kernel(*refs):
        turned_ref = refs[-1]
        for i in range(count):
            if axis == 0:
                turned_ref[i * columns : (i + 1) * columns] = refs[i][...].T
            else:
                turned_ref[:, i * rows : (i + 1) * rows] = refs[i][...].T

    shape = (count * columns, rows) if axis == 0 else (columns, count * rows)
    return run(
        kernel, "turn", [(shape, weights[0].dtype)], weights, after, moved=4 * count * rows * columns
    )[0]


def backward(resid, dec_turned, active_own, active_sibling, row_count):
    height = resid.shape[0]
    latents = active_own.shape[1]

    def kernel(resid_ref, dec_ref, own_ref, sibling_ref, own_grad_ref, total_ref):
        back = jnp.dot(resid_ref[...], dec_ref[...], preferred_element_type=jnp.float32)
        active = jnp.concatenate([own_ref[...], sibling_ref[...]], axis=1)
        code_grad = 2.0 * active * (back + PENALTY / row_count)
        own_grad_ref[...] = code_grad[:, :latents].astype(jnp.bfloat16)
        total_ref[...] = jnp.sum(code_grad, axis=0, keepdims=True)

    return run(
        kernel,
        "backward",
        [((height, latents), jnp.bfloat16), ((1, 2 * latents), jnp.float32)],
        [resid, dec_turned, active_own, active_sibling],
    )


def bias_product(total, enc_weight, own_bias, square, code_sum, row_count):
    latents, width = enc_weight.shape

    def kernel(total_ref, enc_ref, own_ref, square_ref, sum_ref, terms_ref):
        values = total_ref[...]
        high = values.astype(jnp.bfloat16).astype(jnp.float32)
        rest = values - high
        middle = rest.astype(jnp.bfloat16).astype(jnp.float32)
        pieces = [high, middle, rest - middle, jnp.zeros((5, latents), jnp.float32)]
        pieces = jnp.concatenate(pieces, axis=0).astype(jnp.bfloat16)
        product = jnp.dot(pieces, enc_ref[...], preferred_element_type=jnp.float32)
        terms_ref[:, :width] = own_ref[...] - (product[0:1] + (product[1:2] + product[2:3]))
        terms_ref[:, width:] = (square_ref[...] + PENALTY * sum_ref[...]) / row_count

    return run(
        kernel,
        "bias_product",
        [((1, width + LANES), jnp.float32)],
        [total, enc_weight, own_bias, square, code_sum],
    )[0]


def dec_gradient(active_a, active_b, resid_a, resid_b, after):
    half, latents = active_a.shape
    width = resid_a.shape[1]

    def kernel(active_a_ref, active_b_ref, a_ref, b_ref, grad_ref):
        active = jnp.concatenate([active_a_ref[...], active_b_ref[...]], axis=0)
        codes = (active * active).astype(jnp.bfloat16)
        resid = jnp.concatenate([a_ref[...], b_ref[...]], axis=0)
        grad_ref[...] = lax.dot_general(
            codes, resid, CONTRACT_FIRST, preferred_element_type=jnp.float32
        ).astype(jnp.bfloat16)

    return run(
        kernel,
        "dec_gradient",
        [((latents, width), jnp.bfloat16)],
        [active_a, active_b, resid_a, resid_b],
        after,
        flops=4 * half * width * latents,
    )[0]


def enc_gradient(centered_a, centered_b, code_grad_a, resid_b, dec_turned, active_b, total, row_count, stored, after):
    half, width = centered_a.shape
    latents = code_grad_a.shape[1]
    count = len(stored)

    def kernel(*refs):
        a_ref, b_ref, code_grad_a_ref, resid_ref, dec_ref, active_ref, total_ref = refs[:7]
        outs, (grad_ref, bias_ref, sems) = refs[8 + count : 8 + 2 * count], refs[-3:]
        copies = [pltpu.make_async_copy(refs[7 + i], outs[i], sems.at[i]) for i in range(count)]
        for copy in copies:
            copy.start()
        back = jnp.dot(resid_ref[...], dec_ref[:, :latents], preferred_element_type=jnp.float32)
        grad_b = 2.0 * active_ref[...] * (back + PENALTY / row_count)
        bias_ref[...] = total_ref[:, :latents] + jnp.sum(grad_b, axis=0, keepdims=True)
        centered = jnp.concatenate([a_ref[...], b_ref[...]], axis=0)
        code_grad = jnp.concatenate([code_grad_a_ref[...], grad_b.astype(jnp.bfloat16)], axis=0)
        grad_ref[...] = lax.dot_general(
            centered, code_grad, CONTRACT_FIRST, preferred_element_type=jnp.float32
        ).astype(jnp.bfloat16)
        for copy in copies:
            copy.wait()

    *outs, grad, bias = pl.pallas_call(
        kernel,
        out_shape=[jax.ShapeDtypeStruct(a.shape, a.dtype) for a in stored]
        + [vmem((width, latents), jnp.bfloat16), vmem((1, latents), jnp.float32)],
        in_specs=[VMEM] * (8 + count),
        out_specs=[HBM] * count + [VMEM] * 2,
        scratch_shapes=[pltpu.SemaphoreType.DMA((count,))],
        compiler_params=pltpu.CompilerParams(vmem_limit_bytes=LIMIT),
        cost_estimate=pl.CostEstimate(flops=4 * half * latents * width, bytes_accessed=4 * latents * width, transcendentals=0),
        name="enc_gradient",
    )(*[in_vmem(a) for a in (centered_a, centered_b, code_grad_a, resid_b, dec_turned, active_b, total, *stored, after)])
    return outs, grad, bias


def store(arrays, after):
    count = len(arrays)

    def kernel(*refs):
        outs, token_ref, sems = refs[count + 1 : 2 * count + 1], refs[-2], refs[-1]
        copies = [pltpu.make_async_copy(refs[i], outs[i], sems.at[i]) for i in range(count)]
        for copy in copies:
            copy.start()
        token_ref[...] = jnp.zeros_like(token_ref)
        for copy in copies:
            copy.wait()

    return pl.pallas_call(
        kernel,
        out_shape=[jax.ShapeDtypeStruct(a.shape, a.dtype) for a in arrays] + [vmem(*TOKEN)],
        in_specs=[VMEM] * (count + 1),
        out_specs=[HBM] * count + [VMEM],
        scratch_shapes=[pltpu.SemaphoreType.DMA((count,))],
        compiler_params=pltpu.CompilerParams(vmem_limit_bytes=LIMIT),
        cost_estimate=pl.CostEstimate(
            flops=0, bytes_accessed=2 * sum(a.size * a.dtype.itemsize for a in arrays), transcendentals=0
        ),
        name="store",
    )(*[in_vmem(a) for a in (*arrays, after)])


def add(*terms, after=(), order=None):
    order = order or list(range(len(terms)))

    def kernel(*refs):
        values = [refs[order.index(i)][...] for i in range(len(terms))]
        while len(values) > 1:
            values = [left + right for left, right in zip(values[::2], values[1::2])]
        refs[-1][...] = values[0]

    return run(kernel, "add", [(terms[0].shape, jnp.float32)], [terms[i] for i in order], after)[0]


def finish(terms, other, width, after):
    def kernel(terms_ref, other_ref, after_ref, bias_ref, loss_ref):
        total = terms_ref[...] + other_ref[...]
        bias_ref[...] = total[:, :width]
        loss_ref[...] = total[:, width : width + 1] / width

    return pl.pallas_call(
        kernel,
        out_shape=[jax.ShapeDtypeStruct((1, width), jnp.float32), jax.ShapeDtypeStruct((1, 1), jnp.float32)],
        in_specs=[VMEM] * 3,
        out_specs=[VMEM] * 2,
        compiler_params=pltpu.CompilerParams(vmem_limit_bytes=2 << 20),
        name="finish",
    )(in_vmem(terms), in_vmem(other), in_vmem(after))


def local(residuals, enc_weight, enc_bias, dec_weight, dec_bias):
    own_rows, width = residuals.shape
    lat = lax.axis_size("lat")
    row_count = own_rows * lat * lax.axis_size("sub")
    far, steps = plan(lat)

    enc_bias = enc_bias.reshape(1, -1)
    other = swap(residuals, far)
    enc_sibling, dec_sibling = swap(enc_weight, CORES), swap(dec_weight, CORES)
    enc_vmem, own, dec_bias_row = load([enc_weight, residuals, dec_bias.reshape(1, width)])
    paired = stack([own, other], after=[enc_vmem])
    dec_vmem, enc_bias_row = load([dec_weight, enc_bias], after=[paired])
    siblings = enc_sibling, swap(enc_bias_row, CORES), dec_sibling
    rows = gather(paired, steps, ROWS_ORDER, after=[dec_vmem])
    centered_a, active_a, active_sibling, *parts = encode_decode(
        rows, [(enc_vmem, enc_bias_row, dec_vmem), siblings], dec_bias_row, len(steps[-1]) + 1
    )

    summed, dec_turned = halve(parts, steps[::-1], [dec_vmem, siblings[2]])
    active_b = swap(active_sibling, CORES)
    centered_b = swap(centered_a, CORES)
    enc_turned = turn([enc_vmem, siblings[0]], 0, [summed])
    error_args = summed, swap(summed, far), paired, dec_bias_row, row_count
    resid_bf = residual_gradient(*error_args, [enc_turned, active_b, centered_b])

    recon, own_bias, square = own_terms(*error_args, [resid_bf])
    code_total = code_sum(active_a, active_b)
    resid_a = gather(resid_bf, steps, RESID_ORDER, after=[square, code_total])
    resid_b = swap(resid_a, CORES)
    code_grad_a, total = backward(resid_a, dec_turned, active_a, active_sibling, row_count)
    terms = bias_product(total, enc_turned, own_bias, square, code_total, row_count)

    grad_dec = dec_gradient(active_a, active_b, resid_a, resid_b, [terms])
    terms = add(terms, swap(terms, CORES), after=[grad_dec])
    (grad_dec, recon), grad_enc, grad_enc_bias = enc_gradient(
        centered_a, centered_b, code_grad_a, resid_b, dec_turned, active_b, total, row_count, [grad_dec, recon], terms
    )
    for masks in steps:
        terms = add(
            terms,
            *[swap(terms, mask) for mask in masks],
            after=[grad_enc],
            order=[0, *TERMS_ORDER] if len(masks) > 1 else None,
        )
    grad_enc, grad_enc_bias, stored = store([grad_enc, grad_enc_bias], terms)
    grad_dec_bias, loss_value = finish(terms, swap(terms, far), width, stored)
    return recon, loss_value[0], grad_enc, grad_enc_bias[0], grad_dec, grad_dec_bias[0]


def solution(mesh):
    placed = (
        P(("parts", "lat", "sub"), None),
        P(None, ("parts", "lat", "sub")),
        P(("parts", "lat", "sub")),
        P(("parts", "lat", "sub"), None),
        P("parts"),
    )
    return jax.shard_map(
        local,
        mesh=mesh,
        in_specs=placed,
        out_specs=(
            P(("parts", "lat", "sub"), None),
            P("parts"),
            P(None, ("parts", "lat", "sub")),
            P(("parts", "lat", "sub")),
            P(("parts", "lat", "sub"), None),
            P("parts"),
        ),
        check_vma=False,
    )
```
